256 devices in a mesh: dp: 16 (over y_lo, x, core), tensor: 16 (over z, y_hi).
Axes of the slice: x: 4, y: 4 (y_hi: 2, y_lo: 2; y = y_hi * 2 + y_lo), z: 8, core: 2. Of those that a mesh axis runs over, the one named last changes fastest.
Arguments:
- acts: bfloat16 [8192, 2048], P('dp', 'tensor'), may hold values from -6 to 6
- out_grads: bfloat16 [8192, 8192], P('dp', 'tensor'), may hold values from -6 to 6
- basis_out: bfloat16 [8192, 8192], P('tensor'), may hold values from -0.0625 to 0.0625
- basis_in: bfloat16 [2048, 2048], P('tensor'), may hold values from -0.125 to 0.125
- slot_sequence: int32 [32], replicated, may hold values from 0 to 31, each once
- seq_lengths: int32 [32], replicated, may hold values from 1 to 256, 5120 in all
Outputs:
- eigenvalues: float32 [8192, 2048], P('tensor', 'dp')
The draws below stay inside these ranges and needn't reach their ends.
Inputs may be any that keep to these rules, and one draw needn't show every extreme that they name: `slot_sequence`: every sequence number appears exactly once. `seq_lengths`: the largest count is exactly 256.
All inputs are finite; a program needn't handle non-finite values.
Results may differ from the reference program's by a relative error of at most 0.0018.
Values may be sent and summed in bfloat16 or wider, within the bound.
A program may use at most 128 MiB of HBM per device.

```python
import math
import jax
import jax.numpy as jnp
import numpy as np
from jax import lax

DIN = 2048
DOUT = 8192
LEN = 256
NSEQ = 32
TOKENS = 8192


def shard_levels(key, extent, cuts, low, largest):
    factor_of, own = 1.0, jax.random.fold_in(key, 6)
    for position, parts in cuts:
        heights = jnp.exp(jax.random.uniform(jax.random.fold_in(own, position), (parts,), jnp.float32, low / len(cuts), largest / len(cuts)))
        factor_of = factor_of * jnp.repeat(heights, extent[position] // parts).reshape([-1 if axis == position else 1 for axis in range(len(extent))])
    return factor_of


def length_profile(count, total, reach, lean):
    weights = [(1 << 20) // math.isqrt(standing ** lean) + 1 for standing in range(2, count + 1)]
    rest, counts = total - reach - (count - 1), [1] * (count - 1)
    while rest > 0:
        candidates = [i for i in range(count - 1) if counts[i] < reach]
        whole, remaining = sum([weights[i] for i in candidates]), rest
        for i in candidates:
            extra = min(reach - counts[i], max(1, remaining * weights[i] // whole), rest)
            counts[i] = counts[i] + extra
            rest = rest - extra
    return np.array([reach] + counts)


def ragged_sizes(rng, count, total, most, lean):
    if count == 2:
        one = jax.random.randint(rng, (), max(1, total - most), min(most, total - 1) + 1)
        return jnp.stack([one, total - one])
    sizes = jnp.asarray(length_profile(count, total, most, lean), jnp.int32)
    pairs = (count - 1) // 2
    source_of, taker = sizes[1:1 + 2 * pairs:2], sizes[2:2 + 2 * pairs:2]
    room = jnp.minimum(source_of - 1, most - taker)
    moved = jax.random.randint(jax.random.fold_in(rng, 1), (pairs,), 0, 1 << 20) % (room + 1)
    sizes = sizes.at[1:1 + 2 * pairs:2].set(source_of - moved).at[2:2 + 2 * pairs:2].set(taker + moved)
    return sizes[jax.random.permutation(jax.random.fold_in(rng, 2), count)]


def noise(stream_key, dims, width, reach, shards=(), kind=jnp.bfloat16):
    entries = width * jax.random.normal(stream_key, dims, jnp.float32)
    if shards:
        entries = entries * shard_levels(stream_key, dims, shards, -0.22, 0.18)
    return jnp.clip(entries, -reach, reach).astype(kind)


def setup_inputs(seed: int = 0) -> dict:
    keys = jax.random.split(jax.random.key(seed), 7)
    acts = noise(keys[0], (TOKENS, DIN), 1.0, 6.0, ((0, 16), (1, 16)))
    out_grads = noise(keys[1], (TOKENS, DOUT), 1.0, 6.0, ((0, 16), (1, 16)))
    basis_out = noise(keys[2], (DOUT, DOUT), DOUT ** -0.5, 0.0625, ((0, 16),))
    basis_in = noise(keys[3], (DIN, DIN), DIN ** -0.5, 0.125, ((0, 16),))
    slot_sequence = jax.random.permutation(keys[4], NSEQ).astype(jnp.int32)
    seq_lengths = ragged_sizes(keys[5], NSEQ, NSEQ * LEN * 5 // 8, LEN, 2).astype(jnp.int32)
    return dict(acts=acts, out_grads=out_grads, basis_out=basis_out, basis_in=basis_in, slot_sequence=slot_sequence, seq_lengths=seq_lengths)


def reference(acts, out_grads, basis_out, basis_in, slot_sequence, seq_lengths):
    seq_total = seq_lengths.shape[0]
    slot_counts = seq_lengths[slot_sequence]
    positions = jnp.arange(LEN, dtype=jnp.int32)

    def per_slot(running, slot_id):
        first_row = (slot_id * LEN).astype(jnp.int32)
        act_block = lax.dynamic_slice_in_dim(acts, first_row, LEN, 0)
        grad_block = lax.dynamic_slice_in_dim(out_grads, first_row, LEN, 0)
        valid_mask = positions < slot_counts[slot_id]
        masked = jnp.where(valid_mask[:, None], grad_block, jnp.zeros_like(grad_block))
        rot_grads = jnp.dot(masked, basis_out, preferred_element_type=jnp.float32).astype(jnp.bfloat16)
        rot_acts = jnp.dot(act_block, basis_in, preferred_element_type=jnp.float32).astype(jnp.bfloat16)
        rotated = jnp.dot(rot_grads.T, rot_acts, preferred_element_type=jnp.float32)
        return running + rotated * rotated, None

    start_sum = jnp.zeros((DOUT, DIN), jnp.float32)
    summed, _ = lax.scan(per_slot, start_sum, jnp.arange(seq_total, dtype=jnp.int32))
    return summed / (seq_total * LEN)
```

```python
import jax
import jax.numpy as jnp
from jax import lax
from jax.experimental import pallas as pl
from jax.experimental.pallas import tpu as pltpu
from jax.sharding import PartitionSpec as P

LEN = 256
MESH = pl.DeviceIdType.MESH
F32, BF16 = jnp.float32, jnp.bfloat16
ORDER = (4, 3, -3, 2, -2, 1, -1, 0)
GROUPS = ((0, 1), (1, 3), (3, 5), (5, 7), (7, 8))
QS = 4


def kernel(
    acts, grads, bout, bin_, slot_seq, seq_len, out,
    g, bo, bp, a, bi, ra, sb, rb, sq, cr, ts, tr,
    loc, g_s, g_r, py_s, py_r, px_s, px_r, pc_s, pc_r,
    az_s, az_r, ay_s, ay_r, bz_s, bz_r, by_s, by_r, bl_s, bl_r,
    bx_s, bx_r, bc_s, bc_r, rs_s, rs_r, cs_s, cs_r, ts_s, ts_r,
):
    d, t = lax.axis_index("dp"), lax.axis_index("tensor")
    yl, x, c = d // 8, (d // 2) % 4, d % 2
    z, yh = t // 2, t % 2

    def dev(dx=0, dz=0, flip_yl=False, flip_c=False, flip_yh=False):
        nyl = 1 - yl if flip_yl else yl
        nc = 1 - c if flip_c else c
        nyh = 1 - yh if flip_yh else yh
        return (nyl * 8 + (x + dx + 4) % 4 * 2 + nc, (z + dz + 8) % 8 * 2 + nyh)

    def remote(src, dst, s, r, to):
        return pltpu.make_async_remote_copy(
            src_ref=src, dst_ref=dst, send_sem=s, recv_sem=r,
            device_id=to, device_id_type=MESH,
        )

    pending = []

    def send(src, dst, s, r, to):
        copy = remote(src, dst, s, r, to)
        copy.start()
        pending.append(copy)

    def arrived(dst, s, r):
        remote(dst, dst, s, r, dev(dz=1)).wait_recv()

    def way(i):
        return 1 - 2 * i

    partners = [dev(dz=1), dev(dz=-1), dev(flip_yh=True), dev(flip_yl=True, flip_yh=True), dev(flip_c=True)]
    partners += [dev(dx=j, flip_yl=u == 1) for u in range(2) for j in range(4) if u or j]
    barrier = pltpu.get_barrier_semaphore()
    for to in partners:
        pl.semaphore_signal(barrier, inc=1, device_id=to, device_id_type=MESH)

    def column(k, h):
        return pl.multiple_of(((z + ORDER[k] + 8) % 8 * 2 + h) * 512, 512)

    blk = yl * 4 + x
    my_cols = pl.multiple_of(d * 128, 128)
    local = [
        pltpu.make_async_copy(acts, a.at[yh, z], loc.at[8]),
        pltpu.make_async_copy(bin_.at[:, pl.ds(my_cols, 128)], bi.at[blk, c, yh, z], loc.at[9]),
        pltpu.make_async_copy(grads, g.at[0], loc.at[10]),
    ]
    local += [pltpu.make_async_copy(bout.at[:, pl.ds(column(k, yh), 512)], bo.at[k], loc.at[k]) for k in range(8)]
    for copy in local:
        copy.start()
    pl.semaphore_wait(barrier, len(partners))

    def bz(i, h):
        ref = bi.at[blk, c, yh, (z - way(i) * h + 8) % 8]
        return ref.at[pl.ds(64 * i, 64)] if h == 4 else ref

    def az(i, h):
        ref = a.at[yh, (z - way(i) * h + 8) % 8]
        return ref.at[pl.ds(256 * i, 256)] if h == 4 else ref

    def half(ref, i, rows, h):
        return ref.at[pl.ds(rows * i, rows)] if h == 4 else ref

    def hop(h):
        for i in range(2):
            to = dev(dz=way(i))
            origin = (z - way(i) * (h - 1) + 8) % 8
            src = bi.at[blk, c, yh, origin] if h > 1 else bin_.at[:, pl.ds(my_cols, 128)]
            send(half(src, i, 64, h), half(bi.at[blk, c, yh, origin], i, 64, h), bz_s.at[i, h - 1], bz_r.at[i, h - 1], to)
        for i in range(2):
            to = dev(dz=way(i))
            origin = (z - way(i) * (h - 1) + 8) % 8
            src = a.at[yh, origin] if h > 1 else acts
            send(half(src, i, 256, h), half(a.at[yh, origin], i, 256, h), az_s.at[i, h - 1], az_r.at[i, h - 1], to)

    def hop_arrived(h):
        for i in range(2):
            arrived(bz(i, h), bz_s.at[i, h - 1], bz_r.at[i, h - 1])
        for i in range(2):
            arrived(az(i, h), az_s.at[i, h - 1], az_r.at[i, h - 1])

    def rows(dx):
        return pl.multiple_of(c * 256 + (x + dx + 4) % 4 * 64, 64)

    def p_first(k):
        row, cut = rows(0), pl.ds(column(k, 1 - yh), 512)
        to = dev(flip_yl=True, flip_yh=True)
        send(bout.at[pl.ds(row, 64), cut], bp.at[k, pl.ds(row, 64)], py_s.at[k], py_r.at[k], to)

    def p_x(n):
        lo, hi = GROUPS[n]
        for k in range(lo, hi):
            arrived(bp.at[k, pl.ds(rows(0), 64)], py_s.at[k], py_r.at[k])
        ref = bp.at[pl.ds(lo, hi - lo), pl.ds(rows(0), 64)]
        for i in range(2):
            send(ref, ref, px_s.at[n, i], px_r.at[n, i], dev(dx=way(i)))

    def p_relay(n):
        lo, hi = GROUPS[n]
        for i in range(2):
            row = rows(-way(i))
            arrived(bp.at[pl.ds(lo, hi - lo), pl.ds(row, 64)], px_s.at[n, i], px_r.at[n, i])
            ref = bp.at[pl.ds(lo, hi - lo), pl.ds(row + 32 * i, 32)]
            send(ref, ref, px_s.at[n, 2 + i], px_r.at[n, 2 + i], dev(dx=way(i)))

    def p_core(n):
        lo, hi = GROUPS[n]
        for i in range(2):
            ref = bp.at[pl.ds(lo, hi - lo), pl.ds(rows(2) + 32 * i, 32)]
            arrived(ref, px_s.at[n, 2 + i], px_r.at[n, 2 + i])
        ref = bp.at[pl.ds(lo, hi - lo), pl.ds(pl.multiple_of(c * 256, 256), 256)]
        send(ref, ref, pc_s.at[n], pc_r.at[n], dev(flip_c=True))

    def p_ready(n):
        lo, hi = GROUPS[n]
        ref = bp.at[pl.ds(lo, hi - lo), pl.ds(pl.multiple_of((1 - c) * 256, 256), 256)]
        arrived(ref, pc_s.at[n], pc_r.at[n])

    def b_of(u, dx):
        return (1 - yl if u else yl) * 4 + (x + dx + 4) % 4

    def b_start(u):
        ref = bi.at[b_of(u, 0), c]
        for i in range(2):
            send(ref, ref, bx_s.at[u, i], bx_r.at[u, i], dev(dx=way(i)))
        send(ref, ref, bc_s.at[u, 0], bc_r.at[u, 0], dev(flip_c=True))

    def b_relay(u):
        for i in range(2):
            ref = bi.at[b_of(u, -way(i)), c]
            arrived(ref, bx_s.at[u, i], bx_r.at[u, i])
            part = bi.at[b_of(u, -way(i)), c, i]
            send(part, part, bx_s.at[u, 2 + i], bx_r.at[u, 2 + i], dev(dx=way(i)))
            send(ref, ref, bc_s.at[u, 1 + i], bc_r.at[u, 1 + i], dev(flip_c=True))

    def b_last(u):
        for i in range(2):
            arrived(bi.at[b_of(u, 2), c, i], bx_s.at[u, 2 + i], bx_r.at[u, 2 + i])
        ref = bi.at[b_of(u, 2), c]
        send(ref, ref, bc_s.at[u, 3], bc_r.at[u, 3], dev(flip_c=True))

    def rotate(u, n):
        b = b_of(u, (0, -1, 1, 2)[n])
        arrived(bi.at[b, 1 - c], bc_s.at[u, n], bc_r.at[u, n])

        def tile(i, carry):
            row = pl.multiple_of(i * 128, 128)
            left = jnp.concatenate([a[k // 8, k % 8, pl.ds(row, 128), :] for k in range(16)], axis=1)
            right = jnp.concatenate([bi[b, e].reshape(2048, 128) for e in range(2)], axis=1)
            count = seq_len[slot_seq[d * 2 + i // 2]]
            place = lax.broadcasted_iota(jnp.int32, (128, 256), 0) + (i % 2) * 128
            rot = jnp.dot(left, right, preferred_element_type=F32)
            ra[b, pl.ds(row, 128), :] = jnp.where(place < count, rot, 0.0).astype(BF16)
            return carry

        lax.fori_loop(0, 4, tile, 0)

    def product(k, q, lo=0, n=512):
        cut = pl.ds(pl.multiple_of(q * 128, 128), 128)
        own = jnp.dot(g[0, pl.ds(lo, n), :], bo[k, :, cut], preferred_element_type=F32)
        return own + jnp.dot(g[1, pl.ds(lo, n), :], bp[k, :, cut], preferred_element_type=F32)

    def part(ref, i, s, q):
        return ref.at[0, s, q, pl.ds(256 * i, 256)] if s == 0 else ref.at[i, s, q]

    def rs_copy(i, s, q):
        return remote(part(sb, i, s, q), part(rb, i, s, q), rs_s.at[i, s, q], rs_r.at[i, s, q], dev(dz=way(i)))

    def rs_arrived(i, s, q):
        arrived(part(rb, i, s, q), rs_s.at[i, s, q], rs_r.at[i, s, q])

    def stage(s, q):
        if s == 0:
            sb[0, 0, q] = product(0, q).astype(BF16)
            for i in range(2):
                rs_copy(i, 0, q).start()
            return
        for i in range(2):
            rs_arrived(i, s - 1, q)
            k = 2 * s - 1 + i
            if s == 1:
                lo, no = 256 * i, 256 * (1 - i)
                with_sum = product(k, q, lo, 256) + rb[0, 0, q, pl.ds(lo, 256), :].astype(F32)
                sb[i, s, q, pl.ds(lo, 256), :] = with_sum.astype(BF16)
                sb[i, s, q, pl.ds(no, 256), :] = product(k, q, no, 256).astype(BF16)
            else:
                sb[i, s, q] = (product(k, q) + rb[i, s - 1, q].astype(F32)).astype(BF16)
            rs_copy(i, s, q).start()

    def stages(s):
        def body(q, carry):
            stage(s, q)
            return carry

        lax.fori_loop(0, QS, body, 0)

    def squares(q):
        for i in range(2):
            rs_arrived(i, 3, q)
        rot = product(7, q) + rb[0, 3, q].astype(F32) + rb[1, 3, q].astype(F32)
        rot = rot.T.astype(BF16)

        def body(b, carry):
            total = None
            for slot in range(2):
                span = slice(slot * LEN, (slot + 1) * LEN)
                r = jnp.dot(rot[:, span], ra[b, span, :], preferred_element_type=F32)
                total = r * r if total is None else total + r * r
            sq[q, 0, b] = total[:, :128]
            sq[q, 1, b] = total[:, 128:]
            return carry

        lax.fori_loop(0, 8, body, 0)
        send(sq.at[q, 1 - c], cr.at[q], cs_s.at[q], cs_r.at[q], dev(flip_c=True))

    others = [(u, j) for u in range(2) for j in range(4) if u or j]

    def spread(q):
        arrived(cr.at[q], cs_s.at[q], cs_r.at[q])

        def body(b, carry):
            ts[q, b] = (sq[q, c, b] + cr[q, b]).astype(BF16)
            return carry

        lax.fori_loop(0, 8, body, 0)
        for u, j in others:
            send(ts.at[q, b_of(u, j)], tr.at[q, blk], ts_s.at[q, u, j], ts_r.at[q, u, j], dev(dx=j, flip_yl=u == 1))

    def finish(q):
        total = sq[q, c, blk] + cr[q, blk]
        for u, j in others:
            b = b_of(u, -j)
            arrived(tr.at[q, b], ts_s.at[q, u, j], ts_r.at[q, u, j])
            total = total + tr[q, b].astype(F32)
        out[pl.ds(q * 128, 128), :] = total * (1.0 / (32 * LEN))

    hop(1)
    send(grads, g.at[1], g_s, g_r, dev(flip_yh=True))
    for k in range(8):
        p_first(k)
    for h in range(1, 5):
        hop_arrived(h)
        if h == 1:
            local[0].wait()
            local[1].wait()
        if h < 4:
            hop(h + 1)
        p_x(h - 1)
        if h > 1:
            p_relay(h - 2)
        if h > 2:
            p_core(h - 3)
    ref = bi.at[blk, c, yh]
    send(ref, ref, by_s, by_r, dev(flip_yh=True))
    for copy in local[2:]:
        copy.wait()
    arrived(g.at[1], g_s, g_r)
    p_ready(0)
    send(a.at[yh], a.at[yh], ay_s, ay_r, dev(flip_yh=True))
    stages(0)
    p_x(4)
    p_relay(3)
    p_core(2)
    arrived(bi.at[blk, c, 1 - yh], by_s, by_r)
    ref = bi.at[blk, c]
    send(ref, ref, bl_s, bl_r, dev(flip_yl=True))
    b_start(0)
    p_ready(1)
    stages(1)
    p_relay(4)
    p_core(3)
    p_core(4)
    b_relay(0)
    arrived(bi.at[b_of(1, 0), c], bl_s, bl_r)
    b_start(1)
    p_ready(2)
    stages(2)
    b_last(0)
    b_relay(1)
    p_ready(3)
    p_ready(4)
    stages(3)
    arrived(a.at[1 - yh], ay_s, ay_r)
    for n in range(4):
        rotate(0, n)
    b_last(1)
    for n in range(4):
        rotate(1, n)
    for q in range(QS + 2):
        if q < QS:
            squares(q)
        if 1 <= q <= QS:
            spread(q - 1)
        if q >= 2:
            finish(q - 2)

    for copy in pending:
        copy.wait_send()
    for s in range(4):
        for i in range(2):

            def left(q, carry, i=i, s=s):
                rs_copy(i, s, q).wait_send()
                return carry

            lax.fori_loop(0, QS, left, 0)


def shards(acts, out_grads, basis_out, basis_in, slot_sequence, seq_lengths):
    sem = pltpu.SemaphoreType.DMA
    any_, smem = pl.BlockSpec(memory_space=pl.ANY), pl.BlockSpec(memory_space=pltpu.SMEM)
    pair = lambda *shape: [sem(shape)] * 2
    return pl.pallas_call(
        kernel,
        name="eigenvalues",
        out_shape=jax.ShapeDtypeStruct((512, 128), F32),
        in_specs=[any_] * 4 + [smem] * 2,
        out_specs=pl.BlockSpec(memory_space=pltpu.VMEM),
        scratch_shapes=[
            pltpu.VMEM((2, 512, 512), BF16),
            pltpu.VMEM((8, 512, 512), BF16),
            pltpu.VMEM((8, 512, 512), BF16),
            pltpu.VMEM((2, 8, 512, 128), BF16),
            pltpu.VMEM((8, 2, 2, 8, 128, 128), BF16),
            pltpu.VMEM((8, 512, 256), BF16),
            pltpu.VMEM((2, 4, QS, 512, 128), BF16),
            pltpu.VMEM((2, 4, QS, 512, 128), BF16),
            pltpu.VMEM((QS, 2, 8, 128, 128), F32),
            pltpu.VMEM((QS, 8, 128, 128), F32),
            pltpu.VMEM((QS, 8, 128, 128), BF16),
            pltpu.VMEM((QS, 8, 128, 128), BF16),
            sem((11,)),
            *[sem, sem],
            *pair(8), *pair(5, 4), *pair(5),
            *pair(2, 4), *[sem, sem], *pair(2, 4), *[sem, sem], *[sem, sem],
            *pair(2, 4), *pair(2, 4), *pair(2, 4, QS), *pair(QS), *pair(QS, 2, 4),
        ],
        compiler_params=pltpu.CompilerParams(
            collective_id=0, has_side_effects=True, vmem_limit_bytes=56 << 20
        ),
        cost_estimate=pl.CostEstimate(flops=10 * 2**30, bytes_accessed=12 << 20, transcendentals=0),
    )(acts, out_grads, basis_out, basis_in, slot_sequence, seq_lengths)


def solution(mesh):
    return jax.shard_map(
        shards,
        mesh=mesh,
        in_specs=(
            P("dp", "tensor"),
            P("dp", "tensor"),
            P("tensor", None),
            P("tensor", None),
            P(),
            P(),
        ),
        out_specs=P("tensor", "dp"),
        check_vma=False,
    )
```

```python
import jax
import jax.numpy as jnp
from jax import lax
from jax.experimental import pallas as pl
from jax.experimental.pallas import tpu as pltpu
from jax.sharding import PartitionSpec as P

LEN = 256
MESH = pl.DeviceIdType.MESH
F32, BF16 = jnp.float32, jnp.bfloat16
ORDER = (4, 3, -3, 2, -2, 1, -1, 0)
GROUPS = ((0, 1), (1, 3), (3, 5), (5, 7), (7, 8))
QS = 4
WORK = (
    ("bhop", 1), ("py", 0), ("ahop", 1), ("py", 1), ("bw", 1), ("py", 2), ("bhop", 2), ("aw", 1), ("g",),
    ("px", 0), ("bw", 2), ("bhop", 3), ("ahop", 2), ("py", 4), ("px", 1), ("px", 2), ("bw", 3), ("pr", 0),
    ("bhop", 4), ("aw", 2), ("px", 4), ("pr", 1), ("pc", 0), ("bw", 4), ("ahop", 3), ("bs", 0, 0), ("pc", 1),
    ("bs", 0, 1), ("by", 0), ("aw", 3), ("pw", 0), ("gw",), ("pr", 2), ("py", 3), ("st", 0, 0), ("ahop", 4),
    ("pc", 2), ("st", 0, 1), ("by", 1), ("pw", 1), ("aw", 4), ("px", 3), ("st", 1, 0), ("ay", 1), ("byw", 0),
    ("rotA", 0), ("bs", 1, 0), ("pr", 4), ("br", 0, 0), ("st", 1, 1), ("br", 0, 1), ("pr", 3), ("pw", 2),
    ("st", 2, 0), ("byw", 1), ("ay", 0), ("rotA", 1), ("pc", 4), ("bs", 1, 1), ("pc", 3), ("st", 2, 1),
    ("pw", 3), ("ayw", 1), ("pw", 4), ("br", 1, 0), ("bl", 0, 1), ("st", 3, 0), ("bl", 0, 0), ("rotA", 2),
    ("br", 1, 1), ("rotA", 3), ("own",), ("bl", 1, 0), ("st", 3, 1), ("ayw", 0), ("rotB", 2), ("bl", 1, 1),
    ("rotB", 0), ("rotB", 3), ("rotB", 1), ("sq", 1), ("sq", 0), ("spr", 1), ("spr", 0), ("sq", 3),
    ("spr", 3), ("sq", 2), ("fin", 1), ("spr", 2), ("fin", 3), ("fin", 0), ("fin", 2),
)


def kernel(
    acts, grads, bout, bin_, slot_seq, seq_len, out,
    g, bo, bp, a, bi, ra, acc, sb, rb, ownp, sq, cr, ts, tr,
    loc, g_s, g_r, py_s, py_r, px_s, px_r, pc_s, pc_r,
    az_s, az_r, ay_s, ay_r, bz_s, bz_r, by_s, by_r,
    bx_s, bx_r, bc_s, bc_r, rs_s, rs_r, cs_s, cs_r, ts_s, ts_r,
):
    d, t = lax.axis_index("dp"), lax.axis_index("tensor")
    yl, x, c = d // 8, (d // 2) % 4, d % 2
    z, yh = t // 2, t % 2

    def dev(dx=0, dz=0, flip_yl=False, flip_c=False, flip_yh=False):
        nyl = 1 - yl if flip_yl else yl
        nc = 1 - c if flip_c else c
        nyh = 1 - yh if flip_yh else yh
        return (nyl * 8 + (x + dx + 4) % 4 * 2 + nc, (z + dz + 8) % 8 * 2 + nyh)

    def remote(src, dst, s, r, to):
        return pltpu.make_async_remote_copy(
            src_ref=src, dst_ref=dst, send_sem=s, recv_sem=r,
            device_id=to, device_id_type=MESH,
        )

    pending = []

    def send(src, dst, s, r, to):
        copy = remote(src, dst, s, r, to)
        copy.start()
        pending.append(copy)

    def arrived(dst, s, r):
        remote(dst, dst, s, r, dev(dz=1)).wait_recv()

    def way(i):
        return 1 - 2 * i

    neighbour = dev(flip_yl=True, flip_yh=True)
    partners = [dev(dz=1), dev(dz=-1), dev(flip_yh=True), neighbour, dev(flip_c=True)]
    others = [(u, j) for u in range(2) for j in range(4) if u or j]
    partners += [dev(dx=j, flip_yl=u == 1) for u, j in others]
    barrier = pltpu.get_barrier_semaphore()
    for to in partners:
        pl.semaphore_signal(barrier, inc=1, device_id=to, device_id_type=MESH)

    def column(k, h):
        return pl.multiple_of(((z + ORDER[k] + 8) % 8 * 2 + h) * 512, 512)

    me = x * 2 + c
    my_cols = pl.multiple_of(me * 256, 256)
    local = [
        pltpu.make_async_copy(acts, a.at[yh, z], loc.at[8]),
        pltpu.make_async_copy(bin_.at[:, pl.ds(my_cols, 256)], bi.at[me, yh, z], loc.at[9]),
        pltpu.make_async_copy(grads, g.at[0], loc.at[10]),
    ]
    local += [pltpu.make_async_copy(bout.at[:, pl.ds(column(k, yh), 512)], bo.at[k], loc.at[k]) for k in range(8)]
    for copy in local:
        copy.start()
    pl.semaphore_wait(barrier, len(partners))

    def half(ref, i, rows, h):
        return ref.at[pl.ds(rows * i, rows)] if h == 4 else ref

    def bhop(h):
        for i in range(2):
            origin = (z - way(i) * (h - 1) + 8) % 8
            src = bi.at[me, yh, origin] if h > 1 else bin_.at[:, pl.ds(my_cols, 256)]
            send(half(src, i, 64, h), half(bi.at[me, yh, origin], i, 64, h), bz_s.at[i, h - 1], bz_r.at[i, h - 1], dev(dz=way(i)))

    def bw(h):
        for i in range(2):
            ref = half(bi.at[me, yh, (z - way(i) * h + 8) % 8], i, 64, h)
            arrived(ref, bz_s.at[i, h - 1], bz_r.at[i, h - 1])
        if h == 4:
            local[1].wait()

    def ahop(h):
        for i in range(2):
            origin = (z - way(i) * (h - 1) + 8) % 8
            src = a.at[yh, origin] if h > 1 else acts
            send(half(src, i, 256, h), half(a.at[yh, origin], i, 256, h), az_s.at[i, h - 1], az_r.at[i, h - 1], dev(dz=way(i)))

    def aw(h):
        for i in range(2):
            ref = half(a.at[yh, (z - way(i) * h + 8) % 8], i, 256, h)
            arrived(ref, az_s.at[i, h - 1], az_r.at[i, h - 1])
        if h == 4:
            local[0].wait()

    def by(v):
        ref = bi.at[me, yh, pl.ds(4 * v, 4)]
        send(ref, ref, by_s.at[v], by_r.at[v], neighbour)

    def byw(v):
        arrived(bi.at[me, 1 - yh, pl.ds(4 * v, 4)], by_s.at[v], by_r.at[v])

    def ay(v):
        ref = a.at[yh, pl.ds(4 * v, 4)]
        send(ref, ref, ay_s.at[v], ay_r.at[v], dev(flip_yh=True))

    def ayw(v):
        arrived(a.at[1 - yh, pl.ds(4 * v, 4)], ay_s.at[v], ay_r.at[v])

    def gsend():
        send(grads, g.at[1], g_s, g_r, dev(flip_yh=True))

    def gw():
        arrived(g.at[1], g_s, g_r)
        for copy in local[2:]:
            copy.wait()

    def rows(dx):
        return pl.multiple_of(c * 256 + (x + dx + 4) % 4 * 64, 64)

    def span(n):
        return pl.ds(GROUPS[n][0], GROUPS[n][1] - GROUPS[n][0])

    def py(n):
        for k in range(*GROUPS[n]):
            row, cut = rows(0), pl.ds(column(k, 1 - yh), 512)
            send(bout.at[pl.ds(row, 64), cut], bp.at[k, pl.ds(row, 64)], py_s.at[k], py_r.at[k], neighbour)

    def px(n):
        for k in range(*GROUPS[n]):
            arrived(bp.at[k, pl.ds(rows(0), 64)], py_s.at[k], py_r.at[k])
        ref = bp.at[span(n), pl.ds(rows(0), 64)]
        for i in range(2):
            send(ref, ref, px_s.at[n, i], px_r.at[n, i], dev(dx=way(i)))

    def pr(n):
        for i in range(2):
            row = rows(-way(i))
            arrived(bp.at[span(n), pl.ds(row, 64)], px_s.at[n, i], px_r.at[n, i])
            ref = bp.at[span(n), pl.ds(row + 32 * i, 32)]
            send(ref, ref, px_s.at[n, 2 + i], px_r.at[n, 2 + i], dev(dx=way(i)))

    def pc(n):
        for i in range(2):
            arrived(bp.at[span(n), pl.ds(rows(2) + 32 * i, 32)], px_s.at[n, 2 + i], px_r.at[n, 2 + i])
        ref = bp.at[span(n), pl.ds(pl.multiple_of(c * 256, 256), 256)]
        send(ref, ref, pc_s.at[n], pc_r.at[n], dev(flip_c=True))

    def pw(n):
        arrived(bp.at[span(n), pl.ds(pl.multiple_of((1 - c) * 256, 256), 256)], pc_s.at[n], pc_r.at[n])

    def block(dx, e):
        return (x + dx + 4) % 4 * 2 + e

    def b_part(dx, e, u, v):
        return bi.at[block(dx, e), 1 - yh if u else yh, pl.ds(4 * v, 4)]

    def to_core(dx, u, v, n):
        ref = b_part(dx, c, u, v)
        send(ref, ref, bc_s.at[u, v, n], bc_r.at[u, v, n], dev(flip_c=True))

    def bs(u, v):
        ref = b_part(0, c, u, v)
        for i in range(2):
            send(ref, ref, bx_s.at[u, v, i], bx_r.at[u, v, i], dev(dx=way(i)))
        to_core(0, u, v, 0)

    def br(u, v):
        for i in range(2):
            ref = b_part(-way(i), c, u, v)
            arrived(ref, bx_s.at[u, v, i], bx_r.at[u, v, i])
            part = ref.at[pl.ds(2 * i, 2)]
            send(part, part, bx_s.at[u, v, 2 + i], bx_r.at[u, v, 2 + i], dev(dx=way(i)))
            to_core(-way(i), u, v, 1 + i)

    def bl(u, v):
        for i in range(2):
            arrived(b_part(2, c, u, v).at[pl.ds(2 * i, 2)], bx_s.at[u, v, 2 + i], bx_r.at[u, v, 2 + i])
        to_core(2, u, v, 3)

    def rot_half(b, h):
        left = jnp.concatenate([a[h, k] for k in range(8)], axis=1)
        return jnp.dot(left, bi[b, h].reshape(1024, 256), preferred_element_type=F32)

    def rot(n, u):
        dx = (0, -1, 1, 2)[n]
        for e in (c, 1 - c):
            b = block(dx, e)
            if e is not c:
                for v in range(2):
                    arrived(b_part(dx, e, u, v), bc_s.at[u, v, n], bc_r.at[u, v, n])
            if u == 0:
                acc[b] = rot_half(b, yh)
            else:
                total = acc[b] + rot_half(b, 1 - yh)
                place = lax.broadcasted_iota(jnp.int32, (LEN, 256), 0)
                for slot in range(2):
                    count = seq_len[slot_seq[d * 2 + slot]]
                    part = total[slot * LEN : (slot + 1) * LEN]
                    ra[b, pl.ds(slot * LEN, LEN), :] = jnp.where(place < count, part, 0.0).astype(BF16)

    def product(k, pair):
        cut = pl.ds(pair * 256, 256)
        own = jnp.dot(g[0], bo[k, :, cut], preferred_element_type=F32)
        return own + jnp.dot(g[1], bp[k, :, cut], preferred_element_type=F32)

    def rs_part(ref, i, s, q):
        return ref.at[0, s, q, pl.ds(256 * i, 256)] if s == 0 else ref.at[i, s, q]

    def rs_send(i, s, q):
        send(rs_part(sb, i, s, q), rs_part(rb, i, s, q), rs_s.at[i, s, q], rs_r.at[i, s, q], dev(dz=way(i)))

    def rs_arrived(i, s, q):
        arrived(rs_part(rb, i, s, q), rs_s.at[i, s, q], rs_r.at[i, s, q])

    def st(s, pair):
        if s == 0:
            total = product(0, pair)
            for e in range(2):
                sb[0, 0, 2 * pair + e] = total[:, e * 128 : (e + 1) * 128].astype(BF16)
            for i in range(2):
                for e in range(2):
                    rs_send(i, 0, 2 * pair + e)
            return
        for i in range(2):
            total = product(2 * s - 1 + i, pair)
            for e in range(2):
                q, mine = 2 * pair + e, total[:, e * 128 : (e + 1) * 128]
                rs_arrived(i, s - 1, q)
                if s == 1:
                    lo, no = 256 * i, 256 * (1 - i)
                    with_sum = mine[lo : lo + 256] + rb[0, 0, q, pl.ds(lo, 256), :].astype(F32)
                    sb[i, s, q, pl.ds(lo, 256), :] = with_sum.astype(BF16)
                    sb[i, s, q, pl.ds(no, 256), :] = mine[no : no + 256].astype(BF16)
                else:
                    sb[i, s, q] = (mine + rb[i, s - 1, q].astype(F32)).astype(BF16)
                rs_send(i, s, q)

    def own():
        for pair in range(2):
            ownp[:, pl.ds(pair * 256, 256)] = product(7, pair)

    blk = yl * 4 + x

    def squares(q):
        for i in range(2):
            rs_arrived(i, 3, q)
        rotated = ownp[:, pl.ds(q * 128, 128)] + rb[0, 3, q].astype(F32) + rb[1, 3, q].astype(F32)
        rotated = rotated.T.astype(BF16)
        for b in range(8):
            total = None
            for slot in range(2):
                rng = slice(slot * LEN, (slot + 1) * LEN)
                r = jnp.dot(rotated[:, rng], ra[b, rng, :], preferred_element_type=F32)
                total = r * r if total is None else total + r * r
            sq[q, 0, b] = total[:, :128]
            sq[q, 1, b] = total[:, 128:]
        send(sq.at[q, 1 - c], cr.at[q], cs_s.at[q], cs_r.at[q], dev(flip_c=True))

    def chip(u, j):
        return (1 - yl if u else yl) * 4 + (x + j + 4) % 4

    def spread(q):
        arrived(cr.at[q], cs_s.at[q], cs_r.at[q])
        for u, j in others:
            b = chip(u, j)
            ts[q, b] = (sq[q, c, b] + cr[q, b]).astype(BF16)
            send(ts.at[q, b], tr.at[q, blk], ts_s.at[q, u, j], ts_r.at[q, u, j], dev(dx=j, flip_yl=u == 1))

    def finish(q):
        total = sq[q, c, blk] + cr[q, blk]
        for u, j in others:
            b = chip(u, -j)
            arrived(tr.at[q, b], ts_s.at[q, u, j], ts_r.at[q, u, j])
            total = total + tr[q, b].astype(F32)
        out[pl.ds(q * 128, 128), :] = total * (1.0 / (32 * LEN))

    steps = dict(
        bhop=bhop, bw=bw, ahop=ahop, aw=aw, by=by, byw=byw, ay=ay, ayw=ayw, g=gsend, gw=gw,
        py=py, px=px, pr=pr, pc=pc, pw=pw, bs=bs, br=br, bl=bl,
        rotA=lambda n: rot(n, 0), rotB=lambda n: rot(n, 1), st=st, own=own,
        sq=squares, spr=spread, fin=finish,
    )
    for name, *what in WORK:
        steps[name](*what)
    for copy in pending:
        copy.wait_send()


def shards(acts, out_grads, basis_out, basis_in, slot_sequence, seq_lengths):
    sem = pltpu.SemaphoreType.DMA
    any_, smem = pl.BlockSpec(memory_space=pl.ANY), pl.BlockSpec(memory_space=pltpu.SMEM)
    pair = lambda *shape: [sem(shape)] * 2
    return pl.pallas_call(
        kernel,
        name="eigenvalues",
        out_shape=jax.ShapeDtypeStruct((512, 128), F32),
        in_specs=[any_] * 4 + [smem] * 2,
        out_specs=pl.BlockSpec(memory_space=pltpu.VMEM),
        scratch_shapes=[
            pltpu.VMEM((2, 512, 512), BF16),
            pltpu.VMEM((8, 512, 512), BF16),
            pltpu.VMEM((8, 512, 512), BF16),
            pltpu.VMEM((2, 8, 512, 128), BF16),
            pltpu.VMEM((8, 2, 8, 128, 256), BF16),
            pltpu.VMEM((8, 512, 256), BF16),
            pltpu.VMEM((8, 512, 256), F32),
            pltpu.VMEM((2, 4, QS, 512, 128), BF16),
            pltpu.VMEM((2, 4, QS, 512, 128), BF16),
            pltpu.VMEM((512, 512), F32),
            pltpu.VMEM((QS, 2, 8, 128, 128), F32),
            pltpu.VMEM((QS, 8, 128, 128), F32),
            pltpu.VMEM((QS, 8, 128, 128), BF16),
            pltpu.VMEM((QS, 8, 128, 128), BF16),
            sem((11,)),
            *[sem, sem],
            *pair(8), *pair(5, 4), *pair(5),
            *pair(2, 4), *pair(2), *pair(2, 4), *pair(2),
            *pair(2, 2, 4), *pair(2, 2, 4), *pair(2, 4, QS), *pair(QS), *pair(QS, 2, 4),
        ],
        compiler_params=pltpu.CompilerParams(
            collective_id=0, has_side_effects=True, vmem_limit_bytes=56 << 20
        ),
        cost_estimate=pl.CostEstimate(flops=10 * 2**30, bytes_accessed=12 << 20, transcendentals=0),
    )(acts, out_grads, basis_out, basis_in, slot_sequence, seq_lengths)


def solution(mesh):
    return jax.shard_map(
        shards,
        mesh=mesh,
        in_specs=(
            P("dp", "tensor"),
            P("dp", "tensor"),
            P("tensor", None),
            P("tensor", None),
            P(),
            P(),
        ),
        out_specs=P("tensor", "dp"),
        check_vma=False,
    )
```

```python
import jax
import jax.numpy as jnp
from jax import lax
from jax.experimental import pallas as pl
from jax.experimental.pallas import tpu as pltpu
from jax.sharding import PartitionSpec as P

LEN = 256
MESH = pl.DeviceIdType.MESH
F32, BF16 = jnp.float32, jnp.bfloat16
ORDER = (4, 3, -3, 2, -2, 1, -1, 0)
GROUPS = ((0, 1), (1, 3), (3, 5), (5, 8))
QS = 4
WORK = (
    ("py", 1), ("ay",), ("bhop", 1), ("py", 2), ("ahop", 0, 1), ("bw", 1), ("py", 0), ("bhop", 2),
    ("aw", 0, 1), ("bw", 2), ("bhop", 3), ("g",), ("py", 3), ("px", 0), ("ahop", 0, 2), ("px", 1), ("bw", 3),
    ("px", 2), ("ayw",), ("ahop", 1, 1), ("aw", 0, 2), ("bhop", 4), ("px", 3), ("ahop", 0, 3), ("pr", 0),
    ("aw", 1, 1), ("ahop", 1, 2), ("aw", 0, 3), ("bw", 4), ("pr", 1), ("ahop", 0, 4), ("pr", 3), ("bs", 0),
    ("pr", 2), ("by",), ("aw", 1, 2), ("ahop", 1, 3), ("gw",), ("pc", 0), ("pw", 0), ("st", 0, 0),
    ("aw", 1, 3), ("pc", 1), ("st", 0, 1), ("pc", 3), ("pw", 1), ("ahop", 1, 4), ("st", 1, 0), ("byw",),
    ("bs", 1), ("aw", 0, 4), ("pc", 2), ("pw", 3), ("st", 1, 1), ("pw", 2), ("st", 2, 0), ("br", 0),
    ("rot", 0, 0), ("own",), ("st", 2, 1), ("aw", 1, 4), ("br", 1), ("rot", 1, 0), ("rot", 0, 1),
    ("st", 3, 0), ("bl", 0), ("rot", 2, 0), ("st", 3, 1), ("bl", 1), ("rot", 1, 1), ("rot", 2, 1),
    ("rot", 3, 0), ("rot", 3, 1), ("sq", 0), ("sq", 1), ("sq", 3), ("spr", 1), ("sq", 2), ("spr", 0),
    ("spr", 3), ("spr", 2), ("mid", 1), ("mid", 3), ("mid", 0), ("mid", 2), ("fin", 1), ("fin", 0),
    ("fin", 3), ("fin", 2),
)


def kernel(
    acts, grads, bout, bin_, slot_seq, seq_len, out,
    g, bo, bp, a, bi, ra, acc, sb, rb, ownp, sq, cr, keep, t1s, t1r, t2s, t2r,
    loc, g_s, g_r, py_s, py_r, px_s, px_r, pc_s, pc_r,
    az_s, az_r, ay_s, ay_r, bz_s, bz_r, by_s, by_r,
    bx_s, bx_r, bc_s, bc_r, rs_s, rs_r, cs_s, cs_r, t1_s, t1_r, t2_s, t2_r,
):
    d, t = lax.axis_index("dp"), lax.axis_index("tensor")
    yl, x, c = d // 8, (d // 2) % 4, d % 2
    z, yh = t // 2, t % 2

    def dev(dx=0, dz=0, flip_yl=False, flip_c=False, flip_yh=False):
        nyl = 1 - yl if flip_yl else yl
        nc = 1 - c if flip_c else c
        nyh = 1 - yh if flip_yh else yh
        return (nyl * 8 + (x + dx + 4) % 4 * 2 + nc, (z + dz + 8) % 8 * 2 + nyh)

    def remote(src, dst, s, r, to):
        return pltpu.make_async_remote_copy(
            src_ref=src, dst_ref=dst, send_sem=s, recv_sem=r,
            device_id=to, device_id_type=MESH,
        )

    pending = []

    def send(src, dst, s, r, to):
        copy = remote(src, dst, s, r, to)
        copy.start()
        pending.append(copy)

    def arrived(dst, s, r):
        remote(dst, dst, s, r, dev(dz=1)).wait_recv()

    def way(i):
        return 1 - 2 * i

    neighbour = dev(flip_yl=True, flip_yh=True)
    partners = [dev(dz=1), dev(dz=-1), dev(flip_yh=True), neighbour, dev(flip_c=True)]
    partners += [dev(dx=j) for j in range(1, 4)] + [dev(flip_yl=True)]
    barrier = pltpu.get_barrier_semaphore()
    for to in partners:
        pl.semaphore_signal(barrier, inc=1, device_id=to, device_id_type=MESH)

    def column(k, h):
        return pl.multiple_of(((z + ORDER[k] + 8) % 8 * 2 + h) * 512, 512)

    me = x * 2 + c
    my_cols = pl.multiple_of(me * 256, 256)
    local = [
        pltpu.make_async_copy(acts, a.at[yh, z], loc.at[8]),
        pltpu.make_async_copy(bin_.at[:, pl.ds(my_cols, 256)], bi.at[me, yh, z], loc.at[9]),
        pltpu.make_async_copy(grads, g.at[0], loc.at[10]),
    ]
    local += [pltpu.make_async_copy(bout.at[:, pl.ds(column(k, yh), 512)], bo.at[k], loc.at[k]) for k in range(8)]
    for copy in local[:2]:
        copy.start()
    pl.semaphore_wait(barrier, len(partners))

    def half(ref, i, rows, h):
        return ref.at[pl.ds(rows * i, rows)] if h == 4 else ref

    def bhop(h):
        for i in range(2):
            origin = (z - way(i) * (h - 1) + 8) % 8
            src = bi.at[me, yh, origin] if h > 1 else bin_.at[:, pl.ds(my_cols, 256)]
            send(half(src, i, 64, h), half(bi.at[me, yh, origin], i, 64, h), bz_s.at[i, h - 1], bz_r.at[i, h - 1], dev(dz=way(i)))

    def bw(h):
        for i in range(2):
            ref = half(bi.at[me, yh, (z - way(i) * h + 8) % 8], i, 64, h)
            arrived(ref, bz_s.at[i, h - 1], bz_r.at[i, h - 1])
        if h == 1:
            for copy in local[2:]:
                copy.start()
        if h == 4:
            local[1].wait()

    def ahop(u, h):
        side = 1 - yh if u else yh
        for i in range(2):
            origin = (z - way(i) * (h - 1) + 8) % 8
            dst = half(a.at[side, origin], i, 256, h)
            src = acts if h == 1 and u == 0 else dst
            send(src, dst, az_s.at[u, i, h - 1], az_r.at[u, i, h - 1], dev(dz=way(i)))

    def aw(u, h):
        side = 1 - yh if u else yh
        for i in range(2):
            ref = half(a.at[side, (z - way(i) * h + 8) % 8], i, 256, h)
            arrived(ref, az_s.at[u, i, h - 1], az_r.at[u, i, h - 1])
        if u == 0 and h == 4:
            local[0].wait()

    def by():
        ref = bi.at[me, yh]
        send(ref, ref, by_s, by_r, neighbour)

    def byw():
        arrived(bi.at[me, 1 - yh], by_s, by_r)

    def ay():
        send(acts, a.at[yh, z], ay_s, ay_r, dev(flip_yh=True))

    def ayw():
        arrived(a.at[1 - yh, z], ay_s, ay_r)

    def gsend():
        send(grads, g.at[1], g_s, g_r, dev(flip_yh=True))

    def gw():
        arrived(g.at[1], g_s, g_r)
        for copy in local[2:]:
            copy.wait()

    def rows(dx):
        return pl.multiple_of(c * 256 + (x + dx + 4) % 4 * 64, 64)

    def span(n):
        return pl.ds(GROUPS[n][0], GROUPS[n][1] - GROUPS[n][0])

    def py(n):
        for k in range(*GROUPS[n]):
            row, cut = rows(0), pl.ds(column(k, 1 - yh), 512)
            send(bout.at[pl.ds(row, 64), cut], bp.at[k, pl.ds(row, 64)], py_s.at[k], py_r.at[k], neighbour)

    def px(n):
        for k in range(*GROUPS[n]):
            arrived(bp.at[k, pl.ds(rows(0), 64)], py_s.at[k], py_r.at[k])
        ref = bp.at[span(n), pl.ds(rows(0), 64)]
        for i in range(2):
            send(ref, ref, px_s.at[n, i], px_r.at[n, i], dev(dx=way(i)))

    def pr(n):
        for i in range(2):
            row = rows(-way(i))
            arrived(bp.at[span(n), pl.ds(row, 64)], px_s.at[n, i], px_r.at[n, i])
            ref = bp.at[span(n), pl.ds(row + 32 * i, 32)]
            send(ref, ref, px_s.at[n, 2 + i], px_r.at[n, 2 + i], dev(dx=way(i)))

    def pc(n):
        for i in range(2):
            arrived(bp.at[span(n), pl.ds(rows(2) + 32 * i, 32)], px_s.at[n, 2 + i], px_r.at[n, 2 + i])
        ref = bp.at[span(n), pl.ds(pl.multiple_of(c * 256, 256), 256)]
        send(ref, ref, pc_s.at[n], pc_r.at[n], dev(flip_c=True))

    def pw(n):
        arrived(bp.at[span(n), pl.ds(pl.multiple_of((1 - c) * 256, 256), 256)], pc_s.at[n], pc_r.at[n])

    def block(dx, e):
        return (x + dx + 4) % 4 * 2 + e

    def b_part(dx, e, u):
        return bi.at[block(dx, e), 1 - yh if u else yh]

    def to_core(dx, u, n):
        ref = b_part(dx, c, u)
        send(ref, ref, bc_s.at[u, n], bc_r.at[u, n], dev(flip_c=True))

    def bs(u):
        ref = b_part(0, c, u)
        for i in range(2):
            send(ref, ref, bx_s.at[u, i], bx_r.at[u, i], dev(dx=way(i)))
        to_core(0, u, 0)

    def br(u):
        for i in range(2):
            ref = b_part(-way(i), c, u)
            arrived(ref, bx_s.at[u, i], bx_r.at[u, i])
            part = ref.at[pl.ds(4 * i, 4)]
            send(part, part, bx_s.at[u, 2 + i], bx_r.at[u, 2 + i], dev(dx=way(i)))
            to_core(-way(i), u, 1 + i)

    def bl(u):
        for i in range(2):
            arrived(b_part(2, c, u).at[pl.ds(4 * i, 4)], bx_s.at[u, 2 + i], bx_r.at[u, 2 + i])
        to_core(2, u, 3)

    def rot_half(b, h):
        left = jnp.concatenate([a[h, k] for k in range(8)], axis=1)
        return jnp.dot(left, bi[b, h].reshape(1024, 256), preferred_element_type=F32)

    def rot(n, u):
        dx = (0, -1, 1, 2)[n]
        for e in (c, 1 - c):
            b = block(dx, e)
            if e is not c:
                arrived(b_part(dx, e, u), bc_s.at[u, n], bc_r.at[u, n])
            if u == 0:
                acc[b] = rot_half(b, yh)
            else:
                total = acc[b] + rot_half(b, 1 - yh)
                place = lax.broadcasted_iota(jnp.int32, (LEN, 256), 0)
                for slot in range(2):
                    count = seq_len[slot_seq[d * 2 + slot]]
                    part = total[slot * LEN : (slot + 1) * LEN]
                    ra[b, pl.ds(slot * LEN, LEN), :] = jnp.where(place < count, part, 0.0).astype(BF16)

    def product(k, pair):
        cut = pl.ds(pair * 256, 256)
        own = jnp.dot(g[0], bo[k, :, cut], preferred_element_type=F32)
        return own + jnp.dot(g[1], bp[k, :, cut], preferred_element_type=F32)

    def rs_part(ref, i, s, q):
        return ref.at[0, s, q, pl.ds(256 * i, 256)] if s == 0 else ref.at[i, s, q]

    def rs_send(i, s, q):
        send(rs_part(sb, i, s, q), rs_part(rb, i, s, q), rs_s.at[i, s, q], rs_r.at[i, s, q], dev(dz=way(i)))

    def rs_arrived(i, s, q):
        arrived(rs_part(rb, i, s, q), rs_s.at[i, s, q], rs_r.at[i, s, q])

    def st(s, pair):
        if s == 0:
            total = product(0, pair)
            for e in range(2):
                sb[0, 0, 2 * pair + e] = total[:, e * 128 : (e + 1) * 128].astype(BF16)
            for i in range(2):
                for e in range(2):
                    rs_send(i, 0, 2 * pair + e)
            return
        for i in range(2):
            total = product(2 * s - 1 + i, pair)
            for e in range(2):
                q, mine = 2 * pair + e, total[:, e * 128 : (e + 1) * 128]
                rs_arrived(i, s - 1, q)
                if s == 1:
                    lo, no = 256 * i, 256 * (1 - i)
                    with_sum = mine[lo : lo + 256] + rb[0, 0, q, pl.ds(lo, 256), :].astype(F32)
                    sb[i, s, q, pl.ds(lo, 256), :] = with_sum.astype(BF16)
                    sb[i, s, q, pl.ds(no, 256), :] = mine[no : no + 256].astype(BF16)
                else:
                    sb[i, s, q] = (mine + rb[i, s - 1, q].astype(F32)).astype(BF16)
                rs_send(i, s, q)

    def own():
        for pair in range(2):
            ownp[:, pl.ds(pair * 256, 256)] = product(7, pair)

    def squares(q):
        for i in range(2):
            rs_arrived(i, 3, q)
        rotated = ownp[:, pl.ds(q * 128, 128)] + rb[0, 3, q].astype(F32) + rb[1, 3, q].astype(F32)
        rotated = rotated.T.astype(BF16)
        for b in range(8):
            total = None
            for slot in range(2):
                rng = slice(slot * LEN, (slot + 1) * LEN)
                r = jnp.dot(rotated[:, rng], ra[b, rng, :], preferred_element_type=F32)
                total = r * r if total is None else total + r * r
            sq[q, 0, b] = total[:, :128]
            sq[q, 1, b] = total[:, 128:]
        send(sq.at[q, 1 - c], cr.at[q], cs_s.at[q], cs_r.at[q], dev(flip_c=True))

    def mine(q, y, x_to):
        b = y * 4 + (x_to + 4) % 4
        return sq[q, c, b] + cr[q, b]

    def at_x(j):
        return (x + j + 4) % 4

    def spread(q):
        arrived(cr.at[q], cs_s.at[q], cs_r.at[q])
        if q % 2 == 0:
            for j in range(1, 4):
                for y in range(2):
                    t1s[q, at_x(j) * 2 + y] = mine(q, y, at_x(j)).astype(BF16)
                send(t1s.at[q, pl.ds(at_x(j) * 2, 2)], t1r.at[q, pl.ds(x * 2, 2)], t1_s.at[q, j], t1_r.at[q, j], dev(dx=j))
        else:
            for k in range(4):
                t1s[q, k] = mine(q, 1 - yl, k).astype(BF16)
            send(t1s.at[q, pl.ds(0, 4)], t1r.at[q, pl.ds(0, 4)], t1_s.at[q, 0], t1_r.at[q, 0], dev(flip_yl=True))

    def middle(q):
        if q % 2 == 0:
            for j in range(1, 4):
                arrived(t1r.at[q, pl.ds(at_x(-j) * 2, 2)], t1_s.at[q, j], t1_r.at[q, j])
            for y in (1 - yl, yl):
                total = mine(q, y, x)
                for j in range(1, 4):
                    total = total + t1r[q, at_x(-j) * 2 + y].astype(F32)
                if y is yl:
                    keep[q] = total
                else:
                    t2s[q, 0] = total.astype(BF16)
                    send(t2s.at[q, 0], t2r.at[q, 0], t2_s.at[q, 0], t2_r.at[q, 0], dev(flip_yl=True))
        else:
            arrived(t1r.at[q, pl.ds(0, 4)], t1_s.at[q, 0], t1_r.at[q, 0])
            for j in range(1, 4):
                t2s[q, at_x(j)] = (mine(q, yl, at_x(j)) + t1r[q, at_x(j)].astype(F32)).astype(BF16)
                send(t2s.at[q, at_x(j)], t2r.at[q, x], t2_s.at[q, j], t2_r.at[q, j], dev(dx=j))
            keep[q] = mine(q, yl, x) + t1r[q, x].astype(F32)

    def finish(q):
        total = keep[q]
        if q % 2 == 0:
            arrived(t2r.at[q, 0], t2_s.at[q, 0], t2_r.at[q, 0])
            total = total + t2r[q, 0].astype(F32)
        else:
            for j in range(1, 4):
                arrived(t2r.at[q, at_x(-j)], t2_s.at[q, j], t2_r.at[q, j])
                total = total + t2r[q, at_x(-j)].astype(F32)
        out[pl.ds(q * 128, 128), :] = total * (1.0 / (32 * LEN))

    steps = dict(
        bhop=bhop, bw=bw, ahop=ahop, aw=aw, by=by, byw=byw, ay=ay, ayw=ayw, g=gsend, gw=gw,
        py=py, px=px, pr=pr, pc=pc, pw=pw, bs=bs, br=br, bl=bl,
        rot=rot, st=st, own=own, sq=squares, spr=spread, mid=middle, fin=finish,
    )
    for name, *what in WORK:
        steps[name](*what)
    for copy in pending:
        copy.wait_send()


def shards(acts, out_grads, basis_out, basis_in, slot_sequence, seq_lengths):
    sem = pltpu.SemaphoreType.DMA
    any_, smem = pl.BlockSpec(memory_space=pl.ANY), pl.BlockSpec(memory_space=pltpu.SMEM)
    pair = lambda *shape: [sem(shape)] * 2
    return pl.pallas_call(
        kernel,
        name="eigenvalues",
        out_shape=jax.ShapeDtypeStruct((512, 128), F32),
        in_specs=[any_] * 4 + [smem] * 2,
        out_specs=pl.BlockSpec(memory_space=pltpu.VMEM),
        scratch_shapes=[
            pltpu.VMEM((2, 512, 512), BF16),
            pltpu.VMEM((8, 512, 512), BF16),
            pltpu.VMEM((8, 512, 512), BF16),
            pltpu.VMEM((2, 8, 512, 128), BF16),
            pltpu.VMEM((8, 2, 8, 128, 256), BF16),
            pltpu.VMEM((8, 512, 256), BF16),
            pltpu.VMEM((8, 512, 256), F32),
            pltpu.VMEM((2, 4, QS, 512, 128), BF16),
            pltpu.VMEM((2, 4, QS, 512, 128), BF16),
            pltpu.VMEM((512, 512), F32),
            pltpu.VMEM((QS, 2, 8, 128, 128), F32),
            pltpu.VMEM((QS, 8, 128, 128), F32),
            pltpu.VMEM((QS, 128, 128), F32),
            pltpu.VMEM((QS, 8, 128, 128), BF16),
            pltpu.VMEM((QS, 8, 128, 128), BF16),
            pltpu.VMEM((QS, 4, 128, 128), BF16),
            pltpu.VMEM((QS, 4, 128, 128), BF16),
            sem((11,)),
            *[sem, sem],
            *pair(8), *pair(4, 4), *pair(4),
            *pair(2, 2, 4), *[sem, sem], *pair(2, 4), *[sem, sem],
            *pair(2, 4), *pair(2, 4), *pair(2, 4, QS), *pair(QS), *pair(QS, 4), *pair(QS, 4),
        ],
        compiler_params=pltpu.CompilerParams(
            collective_id=0, has_side_effects=True, vmem_limit_bytes=56 << 20
        ),
        cost_estimate=pl.CostEstimate(flops=10 * 2**30, bytes_accessed=12 << 20, transcendentals=0),
    )(acts, out_grads, basis_out, basis_in, slot_sequence, seq_lengths)


def solution(mesh):
    return jax.shard_map(
        shards,
        mesh=mesh,
        in_specs=(
            P("dp", "tensor"),
            P("dp", "tensor"),
            P("tensor", None),
            P("tensor", None),
            P(),
            P(),
        ),
        out_specs=P("tensor", "dp"),
        check_vma=False,
    )
```

```python
import jax
import jax.numpy as jnp
from jax import lax
from jax.experimental import pallas as pl
from jax.experimental.pallas import tpu as pltpu
from jax.sharding import PartitionSpec as P

LEN = 256
MESH = pl.DeviceIdType.MESH
F32, BF16 = jnp.float32, jnp.bfloat16
ORDER = (4, 3, -3, 2, -2, 1, -1, 0)
GROUPS = ((0, 1), (1, 3), (3, 5), (5, 8))
QS = 4
WORK = (
    ("ay",), ("py", 0), ("bhop", 1), ("ahop", 0, 1), ("py", 2), ("py", 1), ("bw", 1), ("bhop", 2), ("py", 3),
    ("ayw",), ("ahop", 1, 1), ("px", 0), ("aw", 0, 1), ("bw", 2), ("bhop", 3), ("g",), ("ahop", 0, 2),
    ("px", 2), ("px", 1), ("bw", 3), ("aw", 1, 1), ("pr", 0), ("bhop", 4), ("ahop", 1, 2), ("aw", 0, 2),
    ("px", 3), ("pr", 2), ("bw", 4), ("pc", 0), ("ahop", 0, 3), ("pr", 1), ("by",), ("aw", 1, 2), ("bs", 0),
    ("ahop", 1, 3), ("pw", 0), ("aw", 0, 3), ("gw",), ("st", 0, 0), ("pc", 1), ("st", 0, 1), ("pr", 3),
    ("pc", 2), ("aw", 1, 3), ("ahop", 0, 4), ("ahop", 1, 4), ("pw", 2), ("pw", 1), ("st", 1, 0), ("byw",),
    ("bs", 1), ("br", 0), ("aw", 0, 4), ("st", 1, 1), ("aw", 1, 4), ("st", 2, 0), ("rot", 2, 0), ("pc", 3),
    ("st", 2, 1), ("pw", 3), ("br", 1), ("rot", 0, 0), ("rot", 1, 0), ("st", 3, 0), ("own",), ("rot", 2, 1),
    ("bl", 0), ("rot", 0, 1), ("st", 3, 1), ("bl", 1), ("rot", 1, 1), ("rot", 3, 0), ("rot", 3, 1), ("sq", 0),
    ("sq", 1), ("sq", 2), ("spr", 0), ("sq", 3), ("spr", 1), ("spr", 2), ("spr", 3), ("mid", 1), ("mid", 0),
    ("mid", 3), ("mid", 2), ("fin", 1), ("fin", 0), ("fin", 2), ("fin", 3),
)


def kernel(
    acts, grads, bout, bin_, slot_seq, seq_len, out,
    g, bo, bp, a, bi, ra, acc, sb, rb, ownp, sq, cr, keep, t1s, t1r, t2s, t2r, t3s, t3r,
    loc, g_s, g_r, py_s, py_r, px_s, px_r, pc_s, pc_r,
    az_s, az_r, ay_s, ay_r, bz_s, bz_r, by_s, by_r,
    bx_s, bx_r, bc_s, bc_r, rs_s, rs_r, cs_s, cs_r, t1_s, t1_r, t2_s, t2_r,
):
    d, t = lax.axis_index("dp"), lax.axis_index("tensor")
    yl, x, c = d // 8, (d // 2) % 4, d % 2
    z, yh = t // 2, t % 2

    def dev(dx=0, dz=0, flip_yl=False, flip_c=False, flip_yh=False):
        nyl = 1 - yl if flip_yl else yl
        nc = 1 - c if flip_c else c
        nyh = 1 - yh if flip_yh else yh
        return (nyl * 8 + (x + dx + 4) % 4 * 2 + nc, (z + dz + 8) % 8 * 2 + nyh)

    def remote(src, dst, s, r, to):
        return pltpu.make_async_remote_copy(
            src_ref=src, dst_ref=dst, send_sem=s, recv_sem=r,
            device_id=to, device_id_type=MESH,
        )

    pending = []

    def send(src, dst, s, r, to):
        copy = remote(src, dst, s, r, to)
        copy.start()
        pending.append(copy)

    def arrived(dst, s, r):
        remote(dst, dst, s, r, dev(dz=1)).wait_recv()

    def way(i):
        return 1 - 2 * i

    neighbour = dev(flip_yl=True, flip_yh=True)
    partners = [dev(dz=1), dev(dz=-1), dev(flip_yh=True), neighbour, dev(flip_c=True)]
    partners += [dev(dx=j) for j in range(1, 4)] + [dev(flip_yl=True)]
    barrier = pltpu.get_barrier_semaphore()
    for to in partners:
        pl.semaphore_signal(barrier, inc=1, device_id=to, device_id_type=MESH)

    def column(k, h):
        return pl.multiple_of(((z + ORDER[k] + 8) % 8 * 2 + h) * 512, 512)

    me = x * 2 + c
    my_cols = pl.multiple_of(me * 256, 256)
    local = [
        pltpu.make_async_copy(acts, a.at[yh, z], loc.at[8]),
        pltpu.make_async_copy(bin_.at[:, pl.ds(my_cols, 256)], bi.at[me, yh, z], loc.at[9]),
        pltpu.make_async_copy(grads, g.at[0], loc.at[10]),
    ]
    local += [pltpu.make_async_copy(bout.at[:, pl.ds(column(k, yh), 512)], bo.at[k], loc.at[k]) for k in range(8)]
    for copy in local[:2]:
        copy.start()
    pl.semaphore_wait(barrier, len(partners))

    def half(ref, i, rows, h):
        return ref.at[pl.ds(rows * i, rows)] if h == 4 else ref

    def bhop(h):
        for i in range(2):
            origin = (z - way(i) * (h - 1) + 8) % 8
            src = bi.at[me, yh, origin] if h > 1 else bin_.at[:, pl.ds(my_cols, 256)]
            send(half(src, i, 64, h), half(bi.at[me, yh, origin], i, 64, h), bz_s.at[i, h - 1], bz_r.at[i, h - 1], dev(dz=way(i)))

    def bw(h):
        for i in range(2):
            ref = half(bi.at[me, yh, (z - way(i) * h + 8) % 8], i, 64, h)
            arrived(ref, bz_s.at[i, h - 1], bz_r.at[i, h - 1])
        if h == 1:
            for copy in local[2:]:
                copy.start()
        if h == 4:
            local[1].wait()

    def ahop(u, h):
        side = 1 - yh if u else yh
        for i in range(2):
            origin = (z - way(i) * (h - 1) + 8) % 8
            dst = half(a.at[side, origin], i, 256, h)
            src = acts if h == 1 and u == 0 else dst
            send(src, dst, az_s.at[u, i, h - 1], az_r.at[u, i, h - 1], dev(dz=way(i)))

    def aw(u, h):
        side = 1 - yh if u else yh
        for i in range(2):
            ref = half(a.at[side, (z - way(i) * h + 8) % 8], i, 256, h)
            arrived(ref, az_s.at[u, i, h - 1], az_r.at[u, i, h - 1])
        if u == 0 and h == 4:
            local[0].wait()

    def by():
        ref = bi.at[me, yh]
        send(ref, ref, by_s, by_r, neighbour)

    def byw():
        arrived(bi.at[me, 1 - yh], by_s, by_r)

    def ay():
        send(acts, a.at[yh, z], ay_s, ay_r, dev(flip_yh=True))

    def ayw():
        arrived(a.at[1 - yh, z], ay_s, ay_r)

    def gsend():
        send(grads, g.at[1], g_s, g_r, dev(flip_yh=True))

    def gw():
        arrived(g.at[1], g_s, g_r)
        for copy in local[2:]:
            copy.wait()

    def rows(dx):
        return pl.multiple_of(c * 256 + (x + dx + 4) % 4 * 64, 64)

    def span(n):
        return pl.ds(GROUPS[n][0], GROUPS[n][1] - GROUPS[n][0])

    def py(n):
        for k in range(*GROUPS[n]):
            row, cut = rows(0), pl.ds(column(k, 1 - yh), 512)
            send(bout.at[pl.ds(row, 64), cut], bp.at[k, pl.ds(row, 64)], py_s.at[k], py_r.at[k], neighbour)

    def px(n):
        for k in range(*GROUPS[n]):
            arrived(bp.at[k, pl.ds(rows(0), 64)], py_s.at[k], py_r.at[k])
        ref = bp.at[span(n), pl.ds(rows(0), 64)]
        for i in range(2):
            send(ref, ref, px_s.at[n, i], px_r.at[n, i], dev(dx=way(i)))

    def pr(n):
        for i in range(2):
            row = rows(-way(i))
            arrived(bp.at[span(n), pl.ds(row, 64)], px_s.at[n, i], px_r.at[n, i])
            ref = bp.at[span(n), pl.ds(row + 32 * i, 32)]
            send(ref, ref, px_s.at[n, 2 + i], px_r.at[n, 2 + i], dev(dx=way(i)))

    def pc(n):
        for i in range(2):
            arrived(bp.at[span(n), pl.ds(rows(2) + 32 * i, 32)], px_s.at[n, 2 + i], px_r.at[n, 2 + i])
        ref = bp.at[span(n), pl.ds(pl.multiple_of(c * 256, 256), 256)]
        send(ref, ref, pc_s.at[n], pc_r.at[n], dev(flip_c=True))

    def pw(n):
        arrived(bp.at[span(n), pl.ds(pl.multiple_of((1 - c) * 256, 256), 256)], pc_s.at[n], pc_r.at[n])

    def block(dx, e):
        return (x + dx + 4) % 4 * 2 + e

    def b_part(dx, e, u):
        return bi.at[block(dx, e), 1 - yh if u else yh]

    def to_core(dx, u, n):
        ref = b_part(dx, c, u)
        send(ref, ref, bc_s.at[u, n], bc_r.at[u, n], dev(flip_c=True))

    def bs(u):
        ref = b_part(0, c, u)
        for i in range(2):
            send(ref, ref, bx_s.at[u, i], bx_r.at[u, i], dev(dx=way(i)))
        to_core(0, u, 0)

    def br(u):
        for i in range(2):
            ref = b_part(-way(i), c, u)
            arrived(ref, bx_s.at[u, i], bx_r.at[u, i])
            part = ref.at[pl.ds(4 * i, 4)]
            send(part, part, bx_s.at[u, 2 + i], bx_r.at[u, 2 + i], dev(dx=way(i)))
            to_core(-way(i), u, 1 + i)

    def bl(u):
        for i in range(2):
            arrived(b_part(2, c, u).at[pl.ds(4 * i, 4)], bx_s.at[u, 2 + i], bx_r.at[u, 2 + i])
        to_core(2, u, 3)

    def rot_half(b, h):
        left = jnp.concatenate([a[h, k] for k in range(8)], axis=1)
        return jnp.dot(left, bi[b, h].reshape(1024, 256), preferred_element_type=F32)

    def rot(n, u):
        dx = (0, -1, 1, 2)[n]
        for e in (c, 1 - c):
            b = block(dx, e)
            if e is not c:
                arrived(b_part(dx, e, u), bc_s.at[u, n], bc_r.at[u, n])
            if u == 0:
                acc[b] = rot_half(b, yh)
            else:
                total = acc[b] + rot_half(b, 1 - yh)
                place = lax.broadcasted_iota(jnp.int32, (LEN, 256), 0)
                for slot in range(2):
                    count = seq_len[slot_seq[d * 2 + slot]]
                    part = total[slot * LEN : (slot + 1) * LEN]
                    ra[b, pl.ds(slot * LEN, LEN), :] = jnp.where(place < count, part, 0.0).astype(BF16)

    def product(k, pair):
        cut = pl.ds(pair * 256, 256)
        own = jnp.dot(g[0], bo[k, :, cut], preferred_element_type=F32)
        return own + jnp.dot(g[1], bp[k, :, cut], preferred_element_type=F32)

    def rs_part(ref, i, s, q):
        return ref.at[0, s, q, pl.ds(256 * i, 256)] if s == 0 else ref.at[i, s, q]

    def rs_send(i, s, q):
        send(rs_part(sb, i, s, q), rs_part(rb, i, s, q), rs_s.at[i, s, q], rs_r.at[i, s, q], dev(dz=way(i)))

    def rs_arrived(i, s, q):
        arrived(rs_part(rb, i, s, q), rs_s.at[i, s, q], rs_r.at[i, s, q])

    def st(s, pair):
        if s == 0:
            total = product(0, pair)
            for e in range(2):
                sb[0, 0, 2 * pair + e] = total[:, e * 128 : (e + 1) * 128].astype(BF16)
            for i in range(2):
                for e in range(2):
                    rs_send(i, 0, 2 * pair + e)
            return
        for i in range(2):
            total = product(2 * s - 1 + i, pair)
            for e in range(2):
                q, mine = 2 * pair + e, total[:, e * 128 : (e + 1) * 128]
                rs_arrived(i, s - 1, q)
                if s == 1:
                    lo, no = 256 * i, 256 * (1 - i)
                    with_sum = mine[lo : lo + 256] + rb[0, 0, q, pl.ds(lo, 256), :].astype(F32)
                    sb[i, s, q, pl.ds(lo, 256), :] = with_sum.astype(BF16)
                    sb[i, s, q, pl.ds(no, 256), :] = mine[no : no + 256].astype(BF16)
                else:
                    sb[i, s, q] = (mine + rb[i, s - 1, q].astype(F32)).astype(BF16)
                rs_send(i, s, q)

    def own():
        for pair in range(2):
            ownp[:, pl.ds(pair * 256, 256)] = product(7, pair)

    def squares(q):
        for i in range(2):
            rs_arrived(i, 3, q)
        rotated = ownp[:, pl.ds(q * 128, 128)] + rb[0, 3, q].astype(F32) + rb[1, 3, q].astype(F32)
        rotated = rotated.T.astype(BF16)
        for b in range(8):
            total = None
            for slot in range(2):
                rng = slice(slot * LEN, (slot + 1) * LEN)
                r = jnp.dot(rotated[:, rng], ra[b, rng, :], preferred_element_type=F32)
                total = r * r if total is None else total + r * r
            sq[q, 0, b] = total[:, :128]
            sq[q, 1, b] = total[:, 128:]
        send(sq.at[q, 1 - c], cr.at[q], cs_s.at[q], cs_r.at[q], dev(flip_c=True))

    def mine(q, y, x_to):
        b = y * 4 + (x_to + 4) % 4
        return sq[q, c, b] + cr[q, b]

    def at_x(j):
        return (x + j + 4) % 4

    def spread(q):
        arrived(cr.at[q], cs_s.at[q], cs_r.at[q])
        if q % 2 == 0:
            for j in range(1, 4):
                for y in range(2):
                    t1s[q, at_x(j) * 2 + y] = mine(q, y, at_x(j)).astype(BF16)
                send(t1s.at[q, pl.ds(at_x(j) * 2, 2)], t1r.at[q, pl.ds(x * 2, 2)], t1_s.at[q, j], t1_r.at[q, j], dev(dx=j))
        else:
            for k in range(4):
                t1s[q, k] = mine(q, 1 - yl, k).astype(BF16)
            send(t1s.at[q, pl.ds(0, 4)], t1r.at[q, pl.ds(0, 4)], t1_s.at[q, 0], t1_r.at[q, 0], dev(flip_yl=True))

    def middle(q):
        if q % 2 == 0:
            for j in range(1, 4):
                arrived(t1r.at[q, pl.ds(at_x(-j) * 2, 2)], t1_s.at[q, j], t1_r.at[q, j])
            for y in (1 - yl, yl):
                total = mine(q, y, x)
                for j in range(1, 4):
                    total = total + t1r[q, at_x(-j) * 2 + y].astype(F32)
                if y is yl:
                    keep[q] = total
                else:
                    t3s[q] = total
                    send(t3s.at[q], t3r.at[q], t2_s.at[q, 0], t2_r.at[q, 0], dev(flip_yl=True))
        else:
            arrived(t1r.at[q, pl.ds(0, 4)], t1_s.at[q, 0], t1_r.at[q, 0])
            for j in range(1, 4):
                t2s[q, at_x(j)] = (mine(q, yl, at_x(j)) + t1r[q, at_x(j)].astype(F32)).astype(BF16)
                send(t2s.at[q, at_x(j)], t2r.at[q, x], t2_s.at[q, j], t2_r.at[q, j], dev(dx=j))
            keep[q] = mine(q, yl, x) + t1r[q, x].astype(F32)

    def finish(q):
        total = keep[q]
        if q % 2 == 0:
            arrived(t3r.at[q], t2_s.at[q, 0], t2_r.at[q, 0])
            total = total + t3r[q]
        else:
            for j in range(1, 4):
                arrived(t2r.at[q, at_x(-j)], t2_s.at[q, j], t2_r.at[q, j])
                total = total + t2r[q, at_x(-j)].astype(F32)
        out[pl.ds(q * 128, 128), :] = total * (1.0 / (32 * LEN))

    steps = dict(
        bhop=bhop, bw=bw, ahop=ahop, aw=aw, by=by, byw=byw, ay=ay, ayw=ayw, g=gsend, gw=gw,
        py=py, px=px, pr=pr, pc=pc, pw=pw, bs=bs, br=br, bl=bl,
        rot=rot, st=st, own=own, sq=squares, spr=spread, mid=middle, fin=finish,
    )
    for name, *what in WORK:
        steps[name](*what)
    for copy in pending:
        copy.wait_send()


def shards(acts, out_grads, basis_out, basis_in, slot_sequence, seq_lengths):
    sem = pltpu.SemaphoreType.DMA
    any_, smem = pl.BlockSpec(memory_space=pl.ANY), pl.BlockSpec(memory_space=pltpu.SMEM)
    pair = lambda *shape: [sem(shape)] * 2
    return pl.pallas_call(
        kernel,
        name="eigenvalues",
        out_shape=jax.ShapeDtypeStruct((512, 128), F32),
        in_specs=[any_] * 4 + [smem] * 2,
        out_specs=pl.BlockSpec(memory_space=pltpu.VMEM),
        scratch_shapes=[
            pltpu.VMEM((2, 512, 512), BF16),
            pltpu.VMEM((8, 512, 512), BF16),
            pltpu.VMEM((8, 512, 512), BF16),
            pltpu.VMEM((2, 8, 512, 128), BF16),
            pltpu.VMEM((8, 2, 8, 128, 256), BF16),
            pltpu.VMEM((8, 512, 256), BF16),
            pltpu.VMEM((8, 512, 256), F32),
            pltpu.VMEM((2, 4, QS, 512, 128), BF16),
            pltpu.VMEM((2, 4, QS, 512, 128), BF16),
            pltpu.VMEM((512, 512), F32),
            pltpu.VMEM((QS, 2, 8, 128, 128), F32),
            pltpu.VMEM((QS, 8, 128, 128), F32),
            pltpu.VMEM((QS, 128, 128), F32),
            pltpu.VMEM((QS, 8, 128, 128), BF16),
            pltpu.VMEM((QS, 8, 128, 128), BF16),
            pltpu.VMEM((QS, 4, 128, 128), BF16),
            pltpu.VMEM((QS, 4, 128, 128), BF16),
            pltpu.VMEM((QS, 128, 128), F32),
            pltpu.VMEM((QS, 128, 128), F32),
            sem((11,)),
            *[sem, sem],
            *pair(8), *pair(4, 4), *pair(4),
            *pair(2, 2, 4), *[sem, sem], *pair(2, 4), *[sem, sem],
            *pair(2, 4), *pair(2, 4), *pair(2, 4, QS), *pair(QS), *pair(QS, 4), *pair(QS, 4),
        ],
        compiler_params=pltpu.CompilerParams(
            collective_id=0, has_side_effects=True, vmem_limit_bytes=56 << 20
        ),
        cost_estimate=pl.CostEstimate(flops=10 * 2**30, bytes_accessed=12 << 20, transcendentals=0),
    )(acts, out_grads, basis_out, basis_in, slot_sequence, seq_lengths)


def solution(mesh):
    return jax.shard_map(
        shards,
        mesh=mesh,
        in_specs=(
            P("dp", "tensor"),
            P("dp", "tensor"),
            P("tensor", None),
            P("tensor", None),
            P(),
            P(),
        ),
        out_specs=P("tensor", "dp"),
        check_vma=False,
    )
```

```python
import jax
import jax.numpy as jnp
from jax import lax
from jax.experimental import pallas as pl
from jax.experimental.pallas import tpu as pltpu
from jax.sharding import PartitionSpec as P

LEN = 256
MESH = pl.DeviceIdType.MESH
F32, BF16 = jnp.float32, jnp.bfloat16
ORDER = (4, 3, -3, 2, -2, 1, -1, 0)
GROUPS = ((0, 1), (1, 3), (3, 5), (5, 8))
QS = 4
WORK = (
    ("py", 0), ("bhop", 1), ("py", 1), ("py", 2), ("ahop", 1), ("g",), ("px", 0), ("bw", 1), ("bhop", 2),
    ("px", 1), ("bw", 2), ("bhop", 3), ("px", 2), ("aw", 1), ("pr", 0), ("py", 3), ("ahop", 2), ("bw", 3),
    ("bhop", 4), ("pr", 1), ("aw", 2), ("pr", 2), ("bw", 4), ("bs", 0, 0), ("ahop", 3), ("by", 0), ("pc", 0),
    ("pw", 0), ("gw",), ("st", 0, 0), ("pc", 1), ("pc", 2), ("by", 1), ("px", 3), ("aw", 3), ("ahop", 4),
    ("pw", 1), ("st", 0, 1), ("bs", 0, 1), ("st", 1, 0), ("pr", 3), ("pw", 2), ("byw", 0), ("aw", 4),
    ("ay", 1), ("bs", 1, 0), ("ay", 0), ("st", 1, 1), ("byw", 1), ("br", 0, 0), ("st", 2, 0), ("pc", 3),
    ("bs", 1, 1), ("rot", 0, 0), ("br", 0, 1), ("st", 2, 1), ("rot", 2, 0), ("rot", 1, 0), ("br", 1, 0),
    ("pw", 3), ("st", 3, 0), ("br", 1, 1), ("bl", 0, 0), ("ayw", 1), ("own",), ("st", 3, 1), ("bl", 0, 1),
    ("ayw", 0), ("rot", 1, 1), ("rot", 2, 1), ("bl", 1, 1), ("bl", 1, 0), ("rot", 0, 1), ("rot", 3, 0),
    ("rot", 3, 1), ("sq", 0), ("sq", 3), ("sq", 1), ("sq", 2), ("spr", 3), ("spr", 0), ("spr", 2), ("spr", 1),
    ("mid", 3), ("mid", 1), ("mid", 0), ("mid", 2), ("fin", 3), ("fin", 0), ("fin", 1), ("fin", 2),
)


def kernel(
    acts, grads, bout, bin_, slot_seq, seq_len, out,
    g, bo, bp, a, bi, ra, acc, sb, rb, ownp, sq, cr, keep, t1s, t1r, t2s, t2r, t3s, t3r,
    loc, g_s, g_r, py_s, py_r, px_s, px_r, pc_s, pc_r,
    az_s, az_r, ay_s, ay_r, bz_s, bz_r, by_s, by_r,
    bx_s, bx_r, bc_s, bc_r, rs_s, rs_r, cs_s, cs_r, t1_s, t1_r, t2_s, t2_r,
):
    d, t = lax.axis_index("dp"), lax.axis_index("tensor")
    yl, x, c = d // 8, (d // 2) % 4, d % 2
    z, yh = t // 2, t % 2

    def dev(dx=0, dz=0, flip_yl=False, flip_c=False, flip_yh=False):
        nyl = 1 - yl if flip_yl else yl
        nc = 1 - c if flip_c else c
        nyh = 1 - yh if flip_yh else yh
        return (nyl * 8 + (x + dx + 4) % 4 * 2 + nc, (z + dz + 8) % 8 * 2 + nyh)

    def remote(src, dst, s, r, to):
        return pltpu.make_async_remote_copy(
            src_ref=src, dst_ref=dst, send_sem=s, recv_sem=r,
            device_id=to, device_id_type=MESH,
        )

    pending = []

    def send(src, dst, s, r, to):
        copy = remote(src, dst, s, r, to)
        copy.start()
        pending.append(copy)

    def arrived(dst, s, r):
        remote(dst, dst, s, r, dev(dz=1)).wait_recv()

    def way(i):
        return 1 - 2 * i

    neighbour = dev(flip_yl=True, flip_yh=True)
    partners = [dev(dz=1), dev(dz=-1), dev(flip_yh=True), neighbour, dev(flip_c=True)]
    partners += [dev(dx=j) for j in range(1, 4)] + [dev(flip_yl=True)]
    barrier = pltpu.get_barrier_semaphore()
    for to in partners:
        pl.semaphore_signal(barrier, inc=1, device_id=to, device_id_type=MESH)

    def column(k, h):
        return pl.multiple_of(((z + ORDER[k] + 8) % 8 * 2 + h) * 512, 512)

    me = x * 2 + c
    my_cols = pl.multiple_of(me * 256, 256)
    local = [
        pltpu.make_async_copy(acts, a.at[yh, z], loc.at[8]),
        pltpu.make_async_copy(bin_.at[:, pl.ds(my_cols, 256)], bi.at[me, yh, z], loc.at[9]),
        pltpu.make_async_copy(grads, g.at[0], loc.at[10]),
    ]
    local += [pltpu.make_async_copy(bout.at[:, pl.ds(column(k, yh), 512)], bo.at[k], loc.at[k]) for k in range(8)]
    for copy in local[:2]:
        copy.start()
    pl.semaphore_wait(barrier, len(partners))

    def half(ref, i, rows, h):
        return ref.at[pl.ds(rows * i, rows)] if h == 4 else ref

    def bhop(h):
        for i in range(2):
            origin = (z - way(i) * (h - 1) + 8) % 8
            src = bi.at[me, yh, origin] if h > 1 else bin_.at[:, pl.ds(my_cols, 256)]
            send(half(src, i, 64, h), half(bi.at[me, yh, origin], i, 64, h), bz_s.at[i, h - 1], bz_r.at[i, h - 1], dev(dz=way(i)))

    def bw(h):
        for i in range(2):
            ref = half(bi.at[me, yh, (z - way(i) * h + 8) % 8], i, 64, h)
            arrived(ref, bz_s.at[i, h - 1], bz_r.at[i, h - 1])
        if h == 1:
            for copy in local[2:]:
                copy.start()
        if h == 4:
            local[1].wait()

    def ahop(h):
        for i in range(2):
            origin = (z - way(i) * (h - 1) + 8) % 8
            src = a.at[yh, origin] if h > 1 else acts
            send(half(src, i, 256, h), half(a.at[yh, origin], i, 256, h), az_s.at[i, h - 1], az_r.at[i, h - 1], dev(dz=way(i)))

    def aw(h):
        for i in range(2):
            ref = half(a.at[yh, (z - way(i) * h + 8) % 8], i, 256, h)
            arrived(ref, az_s.at[i, h - 1], az_r.at[i, h - 1])
        if h == 4:
            local[0].wait()

    def by(v):
        ref = bi.at[me, yh, pl.ds(4 * v, 4)]
        send(ref, ref, by_s.at[v], by_r.at[v], neighbour)

    def byw(v):
        arrived(bi.at[me, 1 - yh, pl.ds(4 * v, 4)], by_s.at[v], by_r.at[v])

    def ay(v):
        ref = a.at[yh, pl.ds(4 * v, 4)]
        send(ref, ref, ay_s.at[v], ay_r.at[v], dev(flip_yh=True))

    def ayw(v):
        arrived(a.at[1 - yh, pl.ds(4 * v, 4)], ay_s.at[v], ay_r.at[v])

    def gsend():
        send(grads, g.at[1], g_s, g_r, dev(flip_yh=True))

    def gw():
        arrived(g.at[1], g_s, g_r)
        for copy in local[2:]:
            copy.wait()

    def rows(dx):
        return pl.multiple_of(c * 256 + (x + dx + 4) % 4 * 64, 64)

    def span(n):
        return pl.ds(GROUPS[n][0], GROUPS[n][1] - GROUPS[n][0])

    def py(n):
        for k in range(*GROUPS[n]):
            row, cut = rows(0), pl.ds(column(k, 1 - yh), 512)
            send(bout.at[pl.ds(row, 64), cut], bp.at[k, pl.ds(row, 64)], py_s.at[k], py_r.at[k], neighbour)

    def px(n):
        for k in range(*GROUPS[n]):
            arrived(bp.at[k, pl.ds(rows(0), 64)], py_s.at[k], py_r.at[k])
        ref = bp.at[span(n), pl.ds(rows(0), 64)]
        for i in range(2):
            send(ref, ref, px_s.at[n, i], px_r.at[n, i], dev(dx=way(i)))

    def pr(n):
        for i in range(2):
            row = rows(-way(i))
            arrived(bp.at[span(n), pl.ds(row, 64)], px_s.at[n, i], px_r.at[n, i])
            ref = bp.at[span(n), pl.ds(row + 32 * i, 32)]
            send(ref, ref, px_s.at[n, 2 + i], px_r.at[n, 2 + i], dev(dx=way(i)))

    def pc(n):
        for i in range(2):
            arrived(bp.at[span(n), pl.ds(rows(2) + 32 * i, 32)], px_s.at[n, 2 + i], px_r.at[n, 2 + i])
        ref = bp.at[span(n), pl.ds(pl.multiple_of(c * 256, 256), 256)]
        send(ref, ref, pc_s.at[n], pc_r.at[n], dev(flip_c=True))

    def pw(n):
        arrived(bp.at[span(n), pl.ds(pl.multiple_of((1 - c) * 256, 256), 256)], pc_s.at[n], pc_r.at[n])

    def block(dx, e):
        return (x + dx + 4) % 4 * 2 + e

    def b_part(dx, e, u, v):
        return bi.at[block(dx, e), 1 - yh if u else yh, pl.ds(4 * v, 4)]

    def to_core(dx, u, v, n):
        ref = b_part(dx, c, u, v)
        send(ref, ref, bc_s.at[u, v, n], bc_r.at[u, v, n], dev(flip_c=True))

    def bs(u, v):
        ref = b_part(0, c, u, v)
        for i in range(2):
            send(ref, ref, bx_s.at[u, v, i], bx_r.at[u, v, i], dev(dx=way(i)))
        to_core(0, u, v, 0)

    def br(u, v):
        for i in range(2):
            ref = b_part(-way(i), c, u, v)
            arrived(ref, bx_s.at[u, v, i], bx_r.at[u, v, i])
            part = ref.at[pl.ds(2 * i, 2)]
            send(part, part, bx_s.at[u, v, 2 + i], bx_r.at[u, v, 2 + i], dev(dx=way(i)))
            to_core(-way(i), u, v, 1 + i)

    def bl(u, v):
        for i in range(2):
            arrived(b_part(2, c, u, v).at[pl.ds(2 * i, 2)], bx_s.at[u, v, 2 + i], bx_r.at[u, v, 2 + i])
        to_core(2, u, v, 3)

    def rot_half(b, h):
        left = jnp.concatenate([a[h, k] for k in range(8)], axis=1)
        return jnp.dot(left, bi[b, h].reshape(1024, 256), preferred_element_type=F32)

    def rot(n, u):
        dx = (0, -1, 1, 2)[n]
        for e in (c, 1 - c):
            b = block(dx, e)
            if e is not c:
                for v in range(2):
                    arrived(b_part(dx, e, u, v), bc_s.at[u, v, n], bc_r.at[u, v, n])
            if u == 0:
                acc[b] = rot_half(b, yh)
            else:
                total = acc[b] + rot_half(b, 1 - yh)
                place = lax.broadcasted_iota(jnp.int32, (LEN, 256), 0)
                for slot in range(2):
                    count = seq_len[slot_seq[d * 2 + slot]]
                    part = total[slot * LEN : (slot + 1) * LEN]
                    ra[b, pl.ds(slot * LEN, LEN), :] = jnp.where(place < count, part, 0.0).astype(BF16)

    def product(k, pair):
        cut = pl.ds(pair * 256, 256)
        own = jnp.dot(g[0], bo[k, :, cut], preferred_element_type=F32)
        return own + jnp.dot(g[1], bp[k, :, cut], preferred_element_type=F32)

    def rs_part(ref, i, s, q):
        return ref.at[0, s, q, pl.ds(256 * i, 256)] if s == 0 else ref.at[i, s, q]

    def rs_send(i, s, q):
        send(rs_part(sb, i, s, q), rs_part(rb, i, s, q), rs_s.at[i, s, q], rs_r.at[i, s, q], dev(dz=way(i)))

    def rs_arrived(i, s, q):
        arrived(rs_part(rb, i, s, q), rs_s.at[i, s, q], rs_r.at[i, s, q])

    def st(s, pair):
        if s == 0:
            total = product(0, pair)
            for e in range(2):
                sb[0, 0, 2 * pair + e] = total[:, e * 128 : (e + 1) * 128].astype(BF16)
            for i in range(2):
                for e in range(2):
                    rs_send(i, 0, 2 * pair + e)
            return
        for i in range(2):
            total = product(2 * s - 1 + i, pair)
            for e in range(2):
                q, mine = 2 * pair + e, total[:, e * 128 : (e + 1) * 128]
                rs_arrived(i, s - 1, q)
                if s == 1:
                    lo, no = 256 * i, 256 * (1 - i)
                    with_sum = mine[lo : lo + 256] + rb[0, 0, q, pl.ds(lo, 256), :].astype(F32)
                    sb[i, s, q, pl.ds(lo, 256), :] = with_sum.astype(BF16)
                    sb[i, s, q, pl.ds(no, 256), :] = mine[no : no + 256].astype(BF16)
                else:
                    sb[i, s, q] = (mine + rb[i, s - 1, q].astype(F32)).astype(BF16)
                rs_send(i, s, q)

    def own():
        for pair in range(2):
            ownp[:, pl.ds(pair * 256, 256)] = product(7, pair)

    def squares(q):
        for i in range(2):
            rs_arrived(i, 3, q)
        rotated = ownp[:, pl.ds(q * 128, 128)] + rb[0, 3, q].astype(F32) + rb[1, 3, q].astype(F32)
        rotated = rotated.T.astype(BF16)
        for b in range(8):
            total = None
            for slot in range(2):
                rng = slice(slot * LEN, (slot + 1) * LEN)
                r = jnp.dot(rotated[:, rng], ra[b, rng, :], preferred_element_type=F32)
                total = r * r if total is None else total + r * r
            sq[q, 0, b] = total[:, :128]
            sq[q, 1, b] = total[:, 128:]
        send(sq.at[q, 1 - c], cr.at[q], cs_s.at[q], cs_r.at[q], dev(flip_c=True))

    def mine(q, y, x_to):
        b = y * 4 + (x_to + 4) % 4
        return sq[q, c, b] + cr[q, b]

    def at_x(j):
        return (x + j + 4) % 4

    def spread(q):
        arrived(cr.at[q], cs_s.at[q], cs_r.at[q])
        if q % 2 == 0:
            for j in range(1, 4):
                for y in range(2):
                    t1s[q, at_x(j) * 2 + y] = mine(q, y, at_x(j)).astype(BF16)
                send(t1s.at[q, pl.ds(at_x(j) * 2, 2)], t1r.at[q, pl.ds(x * 2, 2)], t1_s.at[q, j], t1_r.at[q, j], dev(dx=j))
        else:
            for k in range(4):
                t1s[q, k] = mine(q, 1 - yl, k).astype(BF16)
            send(t1s.at[q, pl.ds(0, 4)], t1r.at[q, pl.ds(0, 4)], t1_s.at[q, 0], t1_r.at[q, 0], dev(flip_yl=True))

    def middle(q):
        if q % 2 == 0:
            for j in range(1, 4):
                arrived(t1r.at[q, pl.ds(at_x(-j) * 2, 2)], t1_s.at[q, j], t1_r.at[q, j])
            for y in (1 - yl, yl):
                total = mine(q, y, x)
                for j in range(1, 4):
                    total = total + t1r[q, at_x(-j) * 2 + y].astype(F32)
                if y is yl:
                    keep[q] = total
                else:
                    t3s[q] = total
                    send(t3s.at[q], t3r.at[q], t2_s.at[q, 0], t2_r.at[q, 0], dev(flip_yl=True))
        else:
            arrived(t1r.at[q, pl.ds(0, 4)], t1_s.at[q, 0], t1_r.at[q, 0])
            for j in range(1, 4):
                t2s[q, at_x(j)] = (mine(q, yl, at_x(j)) + t1r[q, at_x(j)].astype(F32)).astype(BF16)
                send(t2s.at[q, at_x(j)], t2r.at[q, x], t2_s.at[q, j], t2_r.at[q, j], dev(dx=j))
            keep[q] = mine(q, yl, x) + t1r[q, x].astype(F32)

    def finish(q):
        total = keep[q]
        if q % 2 == 0:
            arrived(t3r.at[q], t2_s.at[q, 0], t2_r.at[q, 0])
            total = total + t3r[q]
        else:
            for j in range(1, 4):
                arrived(t2r.at[q, at_x(-j)], t2_s.at[q, j], t2_r.at[q, j])
                total = total + t2r[q, at_x(-j)].astype(F32)
        out[pl.ds(q * 128, 128), :] = total * (1.0 / (32 * LEN))

    steps = dict(
        bhop=bhop, bw=bw, ahop=ahop, aw=aw, by=by, byw=byw, ay=ay, ayw=ayw, g=gsend, gw=gw,
        py=py, px=px, pr=pr, pc=pc, pw=pw, bs=bs, br=br, bl=bl,
        rot=rot, st=st, own=own, sq=squares, spr=spread, mid=middle, fin=finish,
    )
    for name, *what in WORK:
        steps[name](*what)
    for copy in pending:
        copy.wait_send()


def shards(acts, out_grads, basis_out, basis_in, slot_sequence, seq_lengths):
    sem = pltpu.SemaphoreType.DMA
    any_, smem = pl.BlockSpec(memory_space=pl.ANY), pl.BlockSpec(memory_space=pltpu.SMEM)
    pair = lambda *shape: [sem(shape)] * 2
    return pl.pallas_call(
        kernel,
        name="eigenvalues",
        out_shape=jax.ShapeDtypeStruct((512, 128), F32),
        in_specs=[any_] * 4 + [smem] * 2,
        out_specs=pl.BlockSpec(memory_space=pltpu.VMEM),
        scratch_shapes=[
            pltpu.VMEM((2, 512, 512), BF16),
            pltpu.VMEM((8, 512, 512), BF16),
            pltpu.VMEM((8, 512, 512), BF16),
            pltpu.VMEM((2, 8, 512, 128), BF16),
            pltpu.VMEM((8, 2, 8, 128, 256), BF16),
            pltpu.VMEM((8, 512, 256), BF16),
            pltpu.VMEM((8, 512, 256), F32),
            pltpu.VMEM((2, 4, QS, 512, 128), BF16),
            pltpu.VMEM((2, 4, QS, 512, 128), BF16),
            pltpu.VMEM((512, 512), F32),
            pltpu.VMEM((QS, 2, 8, 128, 128), F32),
            pltpu.VMEM((QS, 8, 128, 128), F32),
            pltpu.VMEM((QS, 128, 128), F32),
            pltpu.VMEM((QS, 8, 128, 128), BF16),
            pltpu.VMEM((QS, 8, 128, 128), BF16),
            pltpu.VMEM((QS, 4, 128, 128), BF16),
            pltpu.VMEM((QS, 4, 128, 128), BF16),
            pltpu.VMEM((QS, 128, 128), F32),
            pltpu.VMEM((QS, 128, 128), F32),
            sem((11,)),
            *[sem, sem],
            *pair(8), *pair(4, 4), *pair(4),
            *pair(2, 4), *pair(2), *pair(2, 4), *pair(2),
            *pair(2, 2, 4), *pair(2, 2, 4), *pair(2, 4, QS), *pair(QS), *pair(QS, 4), *pair(QS, 4),
        ],
        compiler_params=pltpu.CompilerParams(
            collective_id=0, has_side_effects=True, vmem_limit_bytes=56 << 20
        ),
        cost_estimate=pl.CostEstimate(flops=10 * 2**30, bytes_accessed=12 << 20, transcendentals=0),
    )(acts, out_grads, basis_out, basis_in, slot_sequence, seq_lengths)


def solution(mesh):
    return jax.shard_map(
        shards,
        mesh=mesh,
        in_specs=(
            P("dp", "tensor"),
            P("dp", "tensor"),
            P("tensor", None),
            P("tensor", None),
            P(),
            P(),
        ),
        out_specs=P("tensor", "dp"),
        check_vma=False,
    )
```

```python
import jax
import jax.numpy as jnp
from jax import lax
from jax.experimental import pallas as pl
from jax.experimental.pallas import tpu as pltpu
from jax.sharding import PartitionSpec as P

LEN = 256
MESH = pl.DeviceIdType.MESH
F32, BF16 = jnp.float32, jnp.bfloat16
ORDER = (4, 3, -3, 2, -2, 1, -1, 0)
GROUPS = ((0, 1), (1, 3), (3, 5), (5, 8))
QS = 4
WORK = (
    ("py", 0), ("bhop", 1), ("py", 1), ("ahop", 0, 1), ("py", 2), ("bw", 1), ("ay",), ("bhop", 2), ("px", 0),
    ("px", 1), ("g",), ("bw", 2), ("bhop", 3), ("aw", 0, 1), ("ahop", 0, 2), ("px", 2), ("bw", 3),
    ("bhop", 4), ("pr", 0), ("ayw",), ("ahop", 1, 1), ("pr", 1), ("py", 3), ("pr", 2), ("aw", 0, 2),
    ("ahop", 0, 3), ("bw", 4), ("bs", 0, 0), ("bs", 0, 1), ("by", 0), ("by", 1), ("aw", 1, 1), ("pc", 0),
    ("ahop", 1, 2), ("pw", 0), ("aw", 0, 3), ("ahop", 0, 4), ("gw",), ("st", 0, 0), ("pc", 1), ("st", 0, 1),
    ("px", 3), ("aw", 1, 2), ("ahop", 1, 3), ("pw", 1), ("st", 1, 0), ("pc", 2), ("st", 1, 1), ("byw", 0),
    ("pr", 3), ("byw", 1), ("bs", 1, 0), ("bs", 1, 1), ("br", 0, 0), ("br", 0, 1), ("aw", 1, 3), ("aw", 0, 4),
    ("ah",), ("pw", 2), ("st", 2, 0), ("ahop", 1, 4), ("rot", 0, 0), ("pc", 3), ("pw", 3), ("st", 2, 1),
    ("rot", 2, 0), ("st", 3, 0), ("br", 1, 0), ("br", 1, 1), ("rot", 1, 0), ("own",), ("aw", 1, 4), ("ahw",),
    ("rot", 1, 1), ("st", 3, 1), ("bl", 0, 0), ("bl", 0, 1), ("rot", 2, 1), ("rot", 0, 1), ("bl", 1, 0),
    ("bl", 1, 1), ("rot", 3, 0), ("rot", 3, 1), ("sq", 1), ("sq", 2), ("sq", 0), ("sq", 3), ("spr", 1),
    ("spr", 2), ("spr", 3), ("spr", 0), ("mid", 1), ("mid", 2), ("mid", 3), ("mid", 0), ("fin", 1),
    ("fin", 2), ("fin", 3), ("fin", 0),
)


def kernel(
    acts, grads, bout, bin_, slot_seq, seq_len, out,
    g, bo, bp, a, bi, ra, acc, sb, rb, ownp, sq, cr, keep, t1s, t1r, t2s, t2r, t3s, t3r,
    loc, g_s, g_r, py_s, py_r, px_s, px_r, pc_s, pc_r,
    az_s, az_r, ay_s, ay_r, ah_s, ah_r, bz_s, bz_r, by_s, by_r,
    bx_s, bx_r, bc_s, bc_r, rs_s, rs_r, cs_s, cs_r, t1_s, t1_r, t2_s, t2_r,
):
    d, t = lax.axis_index("dp"), lax.axis_index("tensor")
    yl, x, c = d // 8, (d // 2) % 4, d % 2
    z, yh = t // 2, t % 2

    def dev(dx=0, dz=0, flip_yl=False, flip_c=False, flip_yh=False):
        nyl = 1 - yl if flip_yl else yl
        nc = 1 - c if flip_c else c
        nyh = 1 - yh if flip_yh else yh
        return (nyl * 8 + (x + dx + 4) % 4 * 2 + nc, (z + dz + 8) % 8 * 2 + nyh)

    def remote(src, dst, s, r, to):
        return pltpu.make_async_remote_copy(
            src_ref=src, dst_ref=dst, send_sem=s, recv_sem=r,
            device_id=to, device_id_type=MESH,
        )

    pending = []

    def send(src, dst, s, r, to):
        copy = remote(src, dst, s, r, to)
        copy.start()
        pending.append(copy)

    def arrived(dst, s, r):
        remote(dst, dst, s, r, dev(dz=1)).wait_recv()

    def way(i):
        return 1 - 2 * i

    neighbour = dev(flip_yl=True, flip_yh=True)
    partners = [dev(dz=1), dev(dz=-1), dev(flip_yh=True), neighbour, dev(flip_c=True)]
    partners += [dev(dx=j) for j in range(1, 4)] + [dev(flip_yl=True)]
    barrier = pltpu.get_barrier_semaphore()
    for to in partners:
        pl.semaphore_signal(barrier, inc=1, device_id=to, device_id_type=MESH)

    def column(k, h):
        return pl.multiple_of(((z + ORDER[k] + 8) % 8 * 2 + h) * 512, 512)

    me = x * 2 + c
    my_cols = pl.multiple_of(me * 256, 256)
    local = [
        pltpu.make_async_copy(acts, a.at[yh, z], loc.at[8]),
        pltpu.make_async_copy(bin_.at[:, pl.ds(my_cols, 256)], bi.at[me, yh, z], loc.at[9]),
        pltpu.make_async_copy(grads, g.at[0], loc.at[10]),
    ]
    local += [pltpu.make_async_copy(bout.at[:, pl.ds(column(k, yh), 512)], bo.at[k], loc.at[k]) for k in range(8)]
    for copy in local[:2]:
        copy.start()
    pl.semaphore_wait(barrier, len(partners))

    def half(ref, i, rows, h):
        return ref.at[pl.ds(rows * i, rows)] if h == 4 else ref

    def bhop(h):
        for i in range(2):
            origin = (z - way(i) * (h - 1) + 8) % 8
            src = bi.at[me, yh, origin] if h > 1 else bin_.at[:, pl.ds(my_cols, 256)]
            send(half(src, i, 64, h), half(bi.at[me, yh, origin], i, 64, h), bz_s.at[i, h - 1], bz_r.at[i, h - 1], dev(dz=way(i)))

    def bw(h):
        for i in range(2):
            ref = half(bi.at[me, yh, (z - way(i) * h + 8) % 8], i, 64, h)
            arrived(ref, bz_s.at[i, h - 1], bz_r.at[i, h - 1])
        if h == 1:
            for copy in local[2:]:
                copy.start()
        if h == 4:
            local[1].wait()

    def ahop(u, h):
        side, size = (1 - yh, 256) if u else (yh, 512)
        for i in range(2):
            origin = (z - way(i) * (h - 1) + 8) % 8
            dst = half(a.at[side, origin, pl.ds(0, size)], i, size // 2, h)
            src = acts if h == 1 and u == 0 else dst
            send(src, dst, az_s.at[u, i, h - 1], az_r.at[u, i, h - 1], dev(dz=way(i)))

    def aw(u, h):
        side, size = (1 - yh, 256) if u else (yh, 512)
        for i in range(2):
            ref = half(a.at[side, (z - way(i) * h + 8) % 8, pl.ds(0, size)], i, size // 2, h)
            arrived(ref, az_s.at[u, i, h - 1], az_r.at[u, i, h - 1])
        if u == 0 and h == 4:
            local[0].wait()

    def by(v):
        ref = bi.at[me, yh, pl.ds(4 * v, 4)]
        send(ref, ref, by_s.at[v], by_r.at[v], neighbour)

    def byw(v):
        arrived(bi.at[me, 1 - yh, pl.ds(4 * v, 4)], by_s.at[v], by_r.at[v])

    def ay():
        send(acts.at[pl.ds(0, 256)], a.at[yh, z, pl.ds(0, 256)], ay_s, ay_r, dev(flip_yh=True))

    def ayw():
        arrived(a.at[1 - yh, z, pl.ds(0, 256)], ay_s, ay_r)

    def ah():
        ref = a.at[yh, pl.ds(0, 8), pl.ds(256, 256)]
        send(ref, ref, ah_s, ah_r, dev(flip_yh=True))

    def ahw():
        arrived(a.at[1 - yh, pl.ds(0, 8), pl.ds(256, 256)], ah_s, ah_r)

    def gsend():
        send(grads, g.at[1], g_s, g_r, dev(flip_yh=True))

    def gw():
        arrived(g.at[1], g_s, g_r)
        for copy in local[2:]:
            copy.wait()

    def rows(dx):
        return pl.multiple_of(c * 256 + (x + dx + 4) % 4 * 64, 64)

    def span(n):
        return pl.ds(GROUPS[n][0], GROUPS[n][1] - GROUPS[n][0])

    def py(n):
        for k in range(*GROUPS[n]):
            row, cut = rows(0), pl.ds(column(k, 1 - yh), 512)
            send(bout.at[pl.ds(row, 64), cut], bp.at[k, pl.ds(row, 64)], py_s.at[k], py_r.at[k], neighbour)

    def px(n):
        for k in range(*GROUPS[n]):
            arrived(bp.at[k, pl.ds(rows(0), 64)], py_s.at[k], py_r.at[k])
        ref = bp.at[span(n), pl.ds(rows(0), 64)]
        for i in range(2):
            send(ref, ref, px_s.at[n, i], px_r.at[n, i], dev(dx=way(i)))

    def pr(n):
        for i in range(2):
            row = rows(-way(i))
            arrived(bp.at[span(n), pl.ds(row, 64)], px_s.at[n, i], px_r.at[n, i])
            ref = bp.at[span(n), pl.ds(row + 32 * i, 32)]
            send(ref, ref, px_s.at[n, 2 + i], px_r.at[n, 2 + i], dev(dx=way(i)))

    def pc(n):
        for i in range(2):
            arrived(bp.at[span(n), pl.ds(rows(2) + 32 * i, 32)], px_s.at[n, 2 + i], px_r.at[n, 2 + i])
        ref = bp.at[span(n), pl.ds(pl.multiple_of(c * 256, 256), 256)]
        send(ref, ref, pc_s.at[n], pc_r.at[n], dev(flip_c=True))

    def pw(n):
        arrived(bp.at[span(n), pl.ds(pl.multiple_of((1 - c) * 256, 256), 256)], pc_s.at[n], pc_r.at[n])

    def block(dx, e):
        return (x + dx + 4) % 4 * 2 + e

    def b_part(dx, e, u, v):
        return bi.at[block(dx, e), 1 - yh if u else yh, pl.ds(4 * v, 4)]

    def to_core(dx, u, v, n):
        ref = b_part(dx, c, u, v)
        send(ref, ref, bc_s.at[u, v, n], bc_r.at[u, v, n], dev(flip_c=True))

    def bs(u, v):
        ref = b_part(0, c, u, v)
        for i in range(2):
            send(ref, ref, bx_s.at[u, v, i], bx_r.at[u, v, i], dev(dx=way(i)))
        to_core(0, u, v, 0)

    def br(u, v):
        for i in range(2):
            ref = b_part(-way(i), c, u, v)
            arrived(ref, bx_s.at[u, v, i], bx_r.at[u, v, i])
            part = ref.at[pl.ds(2 * i, 2)]
            send(part, part, bx_s.at[u, v, 2 + i], bx_r.at[u, v, 2 + i], dev(dx=way(i)))
            to_core(-way(i), u, v, 1 + i)

    def bl(u, v):
        for i in range(2):
            arrived(b_part(2, c, u, v).at[pl.ds(2 * i, 2)], bx_s.at[u, v, 2 + i], bx_r.at[u, v, 2 + i])
        to_core(2, u, v, 3)

    def rot_half(b, h):
        left = jnp.concatenate([a[h, k] for k in range(8)], axis=1)
        return jnp.dot(left, bi[b, h].reshape(1024, 256), preferred_element_type=F32)

    def rot(n, u):
        dx = (0, -1, 1, 2)[n]
        for e in (c, 1 - c):
            b = block(dx, e)
            if e is not c:
                for v in range(2):
                    arrived(b_part(dx, e, u, v), bc_s.at[u, v, n], bc_r.at[u, v, n])
            if u == 0:
                acc[b] = rot_half(b, yh)
            else:
                total = acc[b] + rot_half(b, 1 - yh)
                place = lax.broadcasted_iota(jnp.int32, (LEN, 256), 0)
                for slot in range(2):
                    count = seq_len[slot_seq[d * 2 + slot]]
                    part = total[slot * LEN : (slot + 1) * LEN]
                    ra[b, pl.ds(slot * LEN, LEN), :] = jnp.where(place < count, part, 0.0).astype(BF16)

    def product(k, pair):
        cut = pl.ds(pair * 256, 256)
        own = jnp.dot(g[0], bo[k, :, cut], preferred_element_type=F32)
        return own + jnp.dot(g[1], bp[k, :, cut], preferred_element_type=F32)

    def rs_part(ref, i, s, q):
        return ref.at[0, s, q, pl.ds(256 * i, 256)] if s == 0 else ref.at[i, s, q]

    def rs_send(i, s, q):
        send(rs_part(sb, i, s, q), rs_part(rb, i, s, q), rs_s.at[i, s, q], rs_r.at[i, s, q], dev(dz=way(i)))

    def rs_arrived(i, s, q):
        arrived(rs_part(rb, i, s, q), rs_s.at[i, s, q], rs_r.at[i, s, q])

    def st(s, pair):
        if s == 0:
            total = product(0, pair)
            for e in range(2):
                sb[0, 0, 2 * pair + e] = total[:, e * 128 : (e + 1) * 128].astype(BF16)
            for i in range(2):
                for e in range(2):
                    rs_send(i, 0, 2 * pair + e)
            return
        for i in range(2):
            total = product(2 * s - 1 + i, pair)
            for e in range(2):
                q, mine = 2 * pair + e, total[:, e * 128 : (e + 1) * 128]
                rs_arrived(i, s - 1, q)
                if s == 1:
                    lo, no = 256 * i, 256 * (1 - i)
                    with_sum = mine[lo : lo + 256] + rb[0, 0, q, pl.ds(lo, 256), :].astype(F32)
                    sb[i, s, q, pl.ds(lo, 256), :] = with_sum.astype(BF16)
                    sb[i, s, q, pl.ds(no, 256), :] = mine[no : no + 256].astype(BF16)
                else:
                    sb[i, s, q] = (mine + rb[i, s - 1, q].astype(F32)).astype(BF16)
                rs_send(i, s, q)

    def own():
        for pair in range(2):
            ownp[:, pl.ds(pair * 256, 256)] = product(7, pair)

    def squares(q):
        for i in range(2):
            rs_arrived(i, 3, q)
        rotated = ownp[:, pl.ds(q * 128, 128)] + rb[0, 3, q].astype(F32) + rb[1, 3, q].astype(F32)
        rotated = rotated.T.astype(BF16)
        for b in range(8):
            total = None
            for slot in range(2):
                rng = slice(slot * LEN, (slot + 1) * LEN)
                r = jnp.dot(rotated[:, rng], ra[b, rng, :], preferred_element_type=F32)
                total = r * r if total is None else total + r * r
            sq[q, 0, b] = total[:, :128]
            sq[q, 1, b] = total[:, 128:]
        send(sq.at[q, 1 - c], cr.at[q], cs_s.at[q], cs_r.at[q], dev(flip_c=True))

    def mine(q, y, x_to):
        b = y * 4 + (x_to + 4) % 4
        return sq[q, c, b] + cr[q, b]

    def at_x(j):
        return (x + j + 4) % 4

    def spread(q):
        arrived(cr.at[q], cs_s.at[q], cs_r.at[q])
        if q % 2 == 0:
            for j in range(1, 4):
                for y in range(2):
                    t1s[q, at_x(j) * 2 + y] = mine(q, y, at_x(j)).astype(BF16)
                send(t1s.at[q, pl.ds(at_x(j) * 2, 2)], t1r.at[q, pl.ds(x * 2, 2)], t1_s.at[q, j], t1_r.at[q, j], dev(dx=j))
        else:
            for k in range(4):
                t1s[q, k] = mine(q, 1 - yl, k).astype(BF16)
            send(t1s.at[q, pl.ds(0, 4)], t1r.at[q, pl.ds(0, 4)], t1_s.at[q, 0], t1_r.at[q, 0], dev(flip_yl=True))

    def middle(q):
        if q % 2 == 0:
            for j in range(1, 4):
                arrived(t1r.at[q, pl.ds(at_x(-j) * 2, 2)], t1_s.at[q, j], t1_r.at[q, j])
            for y in (1 - yl, yl):
                total = mine(q, y, x)
                for j in range(1, 4):
                    total = total + t1r[q, at_x(-j) * 2 + y].astype(F32)
                if y is yl:
                    keep[q] = total
                else:
                    t3s[q] = total
                    send(t3s.at[q], t3r.at[q], t2_s.at[q, 0], t2_r.at[q, 0], dev(flip_yl=True))
        else:
            arrived(t1r.at[q, pl.ds(0, 4)], t1_s.at[q, 0], t1_r.at[q, 0])
            for j in range(1, 4):
                t2s[q, at_x(j)] = (mine(q, yl, at_x(j)) + t1r[q, at_x(j)].astype(F32)).astype(BF16)
                send(t2s.at[q, at_x(j)], t2r.at[q, x], t2_s.at[q, j], t2_r.at[q, j], dev(dx=j))
            keep[q] = mine(q, yl, x) + t1r[q, x].astype(F32)

    def finish(q):
        total = keep[q]
        if q % 2 == 0:
            arrived(t3r.at[q], t2_s.at[q, 0], t2_r.at[q, 0])
            total = total + t3r[q]
        else:
            for j in range(1, 4):
                arrived(t2r.at[q, at_x(-j)], t2_s.at[q, j], t2_r.at[q, j])
                total = total + t2r[q, at_x(-j)].astype(F32)
        out[pl.ds(q * 128, 128), :] = total * (1.0 / (32 * LEN))

    steps = dict(
        bhop=bhop, bw=bw, ahop=ahop, aw=aw, by=by, byw=byw, ay=ay, ayw=ayw, ah=ah, ahw=ahw, g=gsend, gw=gw,
        py=py, px=px, pr=pr, pc=pc, pw=pw, bs=bs, br=br, bl=bl,
        rot=rot, st=st, own=own, sq=squares, spr=spread, mid=middle, fin=finish,
    )
    for name, *what in WORK:
        steps[name](*what)
    for copy in pending:
        copy.wait_send()


def shards(acts, out_grads, basis_out, basis_in, slot_sequence, seq_lengths):
    sem = pltpu.SemaphoreType.DMA
    any_, smem = pl.BlockSpec(memory_space=pl.ANY), pl.BlockSpec(memory_space=pltpu.SMEM)
    pair = lambda *shape: [sem(shape)] * 2
    return pl.pallas_call(
        kernel,
        name="eigenvalues",
        out_shape=jax.ShapeDtypeStruct((512, 128), F32),
        in_specs=[any_] * 4 + [smem] * 2,
        out_specs=pl.BlockSpec(memory_space=pltpu.VMEM),
        scratch_shapes=[
            pltpu.VMEM((2, 512, 512), BF16),
            pltpu.VMEM((8, 512, 512), BF16),
            pltpu.VMEM((8, 512, 512), BF16),
            pltpu.VMEM((2, 8, 512, 128), BF16),
            pltpu.VMEM((8, 2, 8, 128, 256), BF16),
            pltpu.VMEM((8, 512, 256), BF16),
            pltpu.VMEM((8, 512, 256), F32),
            pltpu.VMEM((2, 4, QS, 512, 128), BF16),
            pltpu.VMEM((2, 4, QS, 512, 128), BF16),
            pltpu.VMEM((512, 512), F32),
            pltpu.VMEM((QS, 2, 8, 128, 128), F32),
            pltpu.VMEM((QS, 8, 128, 128), F32),
            pltpu.VMEM((QS, 128, 128), F32),
            pltpu.VMEM((QS, 8, 128, 128), BF16),
            pltpu.VMEM((QS, 8, 128, 128), BF16),
            pltpu.VMEM((QS, 4, 128, 128), BF16),
            pltpu.VMEM((QS, 4, 128, 128), BF16),
            pltpu.VMEM((QS, 128, 128), F32),
            pltpu.VMEM((QS, 128, 128), F32),
            sem((11,)),
            *[sem, sem],
            *pair(8), *pair(4, 4), *pair(4),
            *pair(2, 2, 4), *[sem] * 4, *pair(2, 4), *pair(2),
            *pair(2, 2, 4), *pair(2, 2, 4), *pair(2, 4, QS), *pair(QS), *pair(QS, 4), *pair(QS, 4),
        ],
        compiler_params=pltpu.CompilerParams(
            collective_id=0, has_side_effects=True, vmem_limit_bytes=56 << 20
        ),
        cost_estimate=pl.CostEstimate(flops=10 * 2**30, bytes_accessed=12 << 20, transcendentals=0),
    )(acts, out_grads, basis_out, basis_in, slot_sequence, seq_lengths)


def solution(mesh):
    return jax.shard_map(
        shards,
        mesh=mesh,
        in_specs=(
            P("dp", "tensor"),
            P("dp", "tensor"),
            P("tensor", None),
            P("tensor", None),
            P(),
            P(),
        ),
        out_specs=P("tensor", "dp"),
        check_vma=False,
    )
```

```python
import jax
import jax.numpy as jnp
from jax import lax
from jax.experimental import pallas as pl
from jax.experimental.pallas import tpu as pltpu
from jax.sharding import PartitionSpec as P

LEN = 256
MESH = pl.DeviceIdType.MESH
F32, BF16 = jnp.float32, jnp.bfloat16
ORDER = (4, 3, -3, 2, -2, 1, -1, 0)
GROUPS = ((0, 1), (1, 3), (3, 5), (5, 8))
QS = 4
WORK = (
    ("py", 0), ("py", 2), ("bhop", 1), ("py", 1), ("ahop", 0, 1), ("bw", 1), ("bhop", 2), ("ay",), ("px", 0),
    ("g",), ("py", 3), ("px", 2), ("bw", 2), ("bhop", 3), ("aw", 0, 1), ("ahop", 0, 2), ("px", 1), ("pr", 0),
    ("bw", 3), ("bhop", 4), ("ayw",), ("ahop", 1, 1), ("pr", 2), ("bw", 4), ("aw", 0, 2), ("pr", 1),
    ("ahop", 0, 3), ("pc", 2), ("aw", 1, 1), ("pc", 0), ("by",), ("ahop", 1, 2), ("bs", 0), ("pc", 1),
    ("aw", 0, 3), ("ahop", 0, 4), ("pw", 0), ("aw", 1, 2), ("ahop", 1, 3), ("gw",), ("st", 0, 0),
    ("aw", 0, 4), ("st", 0, 1), ("px", 3), ("pw", 2), ("br", 0), ("pw", 1), ("aw", 1, 3), ("ahop", 1, 4),
    ("st", 1, 0), ("pr", 3), ("st", 1, 1), ("byw",), ("bs", 1), ("rot", 1, 0), ("st", 2, 0), ("bl", 0),
    ("aw", 1, 4), ("st", 2, 1), ("pc", 3), ("rot", 0, 0), ("pw", 3), ("br", 1), ("st", 3, 0), ("rot", 1, 1),
    ("rot", 0, 1), ("st", 3, 1), ("own",), ("rot", 2, 0), ("bl", 1), ("rot", 2, 1), ("rot", 3, 0),
    ("rot", 3, 1), ("sq", 1), ("sq", 2), ("sq", 0), ("sq", 3), ("spr", 1), ("spr", 2), ("spr", 3), ("spr", 0),
    ("mid", 1), ("mid", 2), ("mid", 3), ("mid", 0), ("fin", 1), ("fin", 2), ("fin", 3), ("fin", 0),
)


def kernel(
    acts, grads, bout, bin_, slot_seq, seq_len, out,
    g, bo, bp, a, bi, ra, acc, sb, rb, ownp, sq, cr, keep, t1s, t1r, t2s, t2r, t3s, t3r,
    loc, g_s, g_r, py_s, py_r, px_s, px_r, pc_s, pc_r,
    az_s, az_r, ay_s, ay_r, bz_s, bz_r, by_s, by_r,
    bx_s, bx_r, bc_s, bc_r, rs_s, rs_r, cs_s, cs_r, t1_s, t1_r, t2_s, t2_r,
):
    d, t = lax.axis_index("dp"), lax.axis_index("tensor")
    yl, x, c = d // 8, (d // 2) % 4, d % 2
    z, yh = t // 2, t % 2

    def dev(dx=0, dz=0, flip_yl=False, flip_c=False, flip_yh=False):
        nyl = 1 - yl if flip_yl else yl
        nc = 1 - c if flip_c else c
        nyh = 1 - yh if flip_yh else yh
        return (nyl * 8 + (x + dx + 4) % 4 * 2 + nc, (z + dz + 8) % 8 * 2 + nyh)

    def remote(src, dst, s, r, to):
        return pltpu.make_async_remote_copy(
            src_ref=src, dst_ref=dst, send_sem=s, recv_sem=r,
            device_id=to, device_id_type=MESH,
        )

    pending = []

    def send(src, dst, s, r, to):
        copy = remote(src, dst, s, r, to)
        copy.start()
        pending.append(copy)

    def arrived(dst, s, r):
        remote(dst, dst, s, r, dev(dz=1)).wait_recv()

    def way(i):
        return 1 - 2 * i

    neighbour = dev(flip_yl=True, flip_yh=True)
    partners = [dev(dz=1), dev(dz=-1), dev(flip_yh=True), neighbour, dev(flip_c=True)]
    partners += [dev(dx=j) for j in range(1, 4)] + [dev(flip_yl=True)]
    barrier = pltpu.get_barrier_semaphore()
    for to in partners:
        pl.semaphore_signal(barrier, inc=1, device_id=to, device_id_type=MESH)

    def column(k, h):
        return pl.multiple_of(((z + ORDER[k] + 8) % 8 * 2 + h) * 512, 512)

    me = x * 2 + c
    my_cols = pl.multiple_of(me * 256, 256)
    local = [
        pltpu.make_async_copy(acts, a.at[yh, z], loc.at[8]),
        pltpu.make_async_copy(bin_.at[:, pl.ds(my_cols, 256)], bi.at[me, yh, z], loc.at[9]),
        pltpu.make_async_copy(grads, g.at[0], loc.at[10]),
    ]
    local += [pltpu.make_async_copy(bout.at[:, pl.ds(column(k, yh), 512)], bo.at[k], loc.at[k]) for k in range(8)]
    for copy in local[:2]:
        copy.start()
    pl.semaphore_wait(barrier, len(partners))

    def half(ref, i, rows, h):
        return ref.at[pl.ds(rows * i, rows)] if h == 4 else ref

    def bhop(h):
        for i in range(2):
            origin = (z - way(i) * (h - 1) + 8) % 8
            src = bi.at[me, yh, origin] if h > 1 else bin_.at[:, pl.ds(my_cols, 256)]
            send(half(src, i, 64, h), half(bi.at[me, yh, origin], i, 64, h), bz_s.at[i, h - 1], bz_r.at[i, h - 1], dev(dz=way(i)))

    def bw(h):
        for i in range(2):
            ref = half(bi.at[me, yh, (z - way(i) * h + 8) % 8], i, 64, h)
            arrived(ref, bz_s.at[i, h - 1], bz_r.at[i, h - 1])
        if h == 1:
            for copy in local[2:]:
                copy.start()
        if h == 4:
            local[1].wait()

    def ahop(u, h):
        side = 1 - yh if u else yh
        for i in range(2):
            origin = (z - way(i) * (h - 1) + 8) % 8
            dst = half(a.at[side, origin], i, 256, h)
            src = acts if h == 1 and u == 0 else dst
            send(src, dst, az_s.at[u, i, h - 1], az_r.at[u, i, h - 1], dev(dz=way(i)))

    def aw(u, h):
        side = 1 - yh if u else yh
        for i in range(2):
            ref = half(a.at[side, (z - way(i) * h + 8) % 8], i, 256, h)
            arrived(ref, az_s.at[u, i, h - 1], az_r.at[u, i, h - 1])
        if u == 0 and h == 4:
            local[0].wait()

    def by():
        ref = bi.at[me, yh]
        send(ref, ref, by_s, by_r, neighbour)

    def byw():
        arrived(bi.at[me, 1 - yh], by_s, by_r)

    def ay():
        send(acts, a.at[yh, z], ay_s, ay_r, dev(flip_yh=True))

    def ayw():
        arrived(a.at[1 - yh, z], ay_s, ay_r)

    def gsend():
        send(grads, g.at[1], g_s, g_r, dev(flip_yh=True))

    def gw():
        arrived(g.at[1], g_s, g_r)
        for copy in local[2:]:
            copy.wait()

    def rows(dx):
        return pl.multiple_of(c * 256 + (x + dx + 4) % 4 * 64, 64)

    def span(n):
        return pl.ds(GROUPS[n][0], GROUPS[n][1] - GROUPS[n][0])

    def py(n):
        for k in range(*GROUPS[n]):
            row, cut = rows(0), pl.ds(column(k, 1 - yh), 512)
            send(bout.at[pl.ds(row, 64), cut], bp.at[k, pl.ds(row, 64)], py_s.at[k], py_r.at[k], neighbour)

    def px(n):
        for k in range(*GROUPS[n]):
            arrived(bp.at[k, pl.ds(rows(0), 64)], py_s.at[k], py_r.at[k])
        ref = bp.at[span(n), pl.ds(rows(0), 64)]
        for i in range(2):
            send(ref, ref, px_s.at[n, i], px_r.at[n, i], dev(dx=way(i)))

    def pr(n):
        for i in range(2):
            row = rows(-way(i))
            arrived(bp.at[span(n), pl.ds(row, 64)], px_s.at[n, i], px_r.at[n, i])
            ref = bp.at[span(n), pl.ds(row + 32 * i, 32)]
            send(ref, ref, px_s.at[n, 2 + i], px_r.at[n, 2 + i], dev(dx=way(i)))

    def pc(n):
        for i in range(2):
            arrived(bp.at[span(n), pl.ds(rows(2) + 32 * i, 32)], px_s.at[n, 2 + i], px_r.at[n, 2 + i])
        ref = bp.at[span(n), pl.ds(pl.multiple_of(c * 256, 256), 256)]
        send(ref, ref, pc_s.at[n], pc_r.at[n], dev(flip_c=True))

    def pw(n):
        arrived(bp.at[span(n), pl.ds(pl.multiple_of((1 - c) * 256, 256), 256)], pc_s.at[n], pc_r.at[n])

    def block(dx, e):
        return (x + dx + 4) % 4 * 2 + e

    def b_part(dx, e, u):
        return bi.at[block(dx, e), 1 - yh if u else yh]

    def to_core(dx, u, n):
        ref = b_part(dx, c, u)
        send(ref, ref, bc_s.at[u, n], bc_r.at[u, n], dev(flip_c=True))

    def bs(u):
        ref = b_part(0, c, u)
        for i in range(2):
            send(ref, ref, bx_s.at[u, i], bx_r.at[u, i], dev(dx=way(i)))
        to_core(0, u, 0)

    def br(u):
        for i in range(2):
            ref = b_part(-way(i), c, u)
            arrived(ref, bx_s.at[u, i], bx_r.at[u, i])
            part = ref.at[pl.ds(4 * i, 4)]
            send(part, part, bx_s.at[u, 2 + i], bx_r.at[u, 2 + i], dev(dx=way(i)))
            to_core(-way(i), u, 1 + i)

    def bl(u):
        for i in range(2):
            arrived(b_part(2, c, u).at[pl.ds(4 * i, 4)], bx_s.at[u, 2 + i], bx_r.at[u, 2 + i])
        to_core(2, u, 3)

    def rot_half(b, h):
        left = jnp.concatenate([a[h, k] for k in range(8)], axis=1)
        return jnp.dot(left, bi[b, h].reshape(1024, 256), preferred_element_type=F32)

    def rot(n, u):
        dx = (0, -1, 1, 2)[n]
        for e in (c, 1 - c):
            b = block(dx, e)
            if e is not c:
                arrived(b_part(dx, e, u), bc_s.at[u, n], bc_r.at[u, n])
            if u == 0:
                acc[b] = rot_half(b, yh)
            else:
                total = acc[b] + rot_half(b, 1 - yh)
                place = lax.broadcasted_iota(jnp.int32, (LEN, 256), 0)
                for slot in range(2):
                    count = seq_len[slot_seq[d * 2 + slot]]
                    part = total[slot * LEN : (slot + 1) * LEN]
                    ra[b, pl.ds(slot * LEN, LEN), :] = jnp.where(place < count, part, 0.0).astype(BF16)

    def product(k, pair):
        cut = pl.ds(pair * 256, 256)
        own = jnp.dot(g[0], bo[k, :, cut], preferred_element_type=F32)
        return own + jnp.dot(g[1], bp[k, :, cut], preferred_element_type=F32)

    def rs_part(ref, i, s, q):
        return ref.at[0, s, q, pl.ds(256 * i, 256)] if s == 0 else ref.at[i, s, q]

    def rs_send(i, s, q):
        send(rs_part(sb, i, s, q), rs_part(rb, i, s, q), rs_s.at[i, s, q], rs_r.at[i, s, q], dev(dz=way(i)))

    def rs_arrived(i, s, q):
        arrived(rs_part(rb, i, s, q), rs_s.at[i, s, q], rs_r.at[i, s, q])

    def st(s, pair):
        if s == 0:
            total = product(0, pair)
            for e in range(2):
                sb[0, 0, 2 * pair + e] = total[:, e * 128 : (e + 1) * 128].astype(BF16)
            for i in range(2):
                for e in range(2):
                    rs_send(i, 0, 2 * pair + e)
            return
        for i in range(2):
            total = product(2 * s - 1 + i, pair)
            for e in range(2):
                q, mine = 2 * pair + e, total[:, e * 128 : (e + 1) * 128]
                rs_arrived(i, s - 1, q)
                if s == 1:
                    lo, no = 256 * i, 256 * (1 - i)
                    with_sum = mine[lo : lo + 256] + rb[0, 0, q, pl.ds(lo, 256), :].astype(F32)
                    sb[i, s, q, pl.ds(lo, 256), :] = with_sum.astype(BF16)
                    sb[i, s, q, pl.ds(no, 256), :] = mine[no : no + 256].astype(BF16)
                else:
                    sb[i, s, q] = (mine + rb[i, s - 1, q].astype(F32)).astype(BF16)
                rs_send(i, s, q)

    def own():
        for pair in range(2):
            ownp[:, pl.ds(pair * 256, 256)] = product(7, pair)

    def squares(q):
        for i in range(2):
            rs_arrived(i, 3, q)
        rotated = ownp[:, pl.ds(q * 128, 128)] + rb[0, 3, q].astype(F32) + rb[1, 3, q].astype(F32)
        rotated = rotated.T.astype(BF16)
        for b in range(8):
            total = None
            for slot in range(2):
                rng = slice(slot * LEN, (slot + 1) * LEN)
                r = jnp.dot(rotated[:, rng], ra[b, rng, :], preferred_element_type=F32)
                total = r * r if total is None else total + r * r
            sq[q, 0, b] = total[:, :128]
            sq[q, 1, b] = total[:, 128:]
        send(sq.at[q, 1 - c], cr.at[q], cs_s.at[q], cs_r.at[q], dev(flip_c=True))

    def mine(q, y, x_to):
        b = y * 4 + (x_to + 4) % 4
        return sq[q, c, b] + cr[q, b]

    def at_x(j):
        return (x + j + 4) % 4

    def spread(q):
        arrived(cr.at[q], cs_s.at[q], cs_r.at[q])
        if q % 2 == 0:
            for j in range(1, 4):
                for y in range(2):
                    t1s[q, at_x(j) * 2 + y] = mine(q, y, at_x(j)).astype(BF16)
                send(t1s.at[q, pl.ds(at_x(j) * 2, 2)], t1r.at[q, pl.ds(x * 2, 2)], t1_s.at[q, j], t1_r.at[q, j], dev(dx=j))
        else:
            for k in range(4):
                t1s[q, k] = mine(q, 1 - yl, k).astype(BF16)
            send(t1s.at[q, pl.ds(0, 4)], t1r.at[q, pl.ds(0, 4)], t1_s.at[q, 0], t1_r.at[q, 0], dev(flip_yl=True))

    def middle(q):
        if q % 2 == 0:
            for j in range(1, 4):
                arrived(t1r.at[q, pl.ds(at_x(-j) * 2, 2)], t1_s.at[q, j], t1_r.at[q, j])
            for y in (1 - yl, yl):
                total = mine(q, y, x)
                for j in range(1, 4):
                    total = total + t1r[q, at_x(-j) * 2 + y].astype(F32)
                if y is yl:
                    keep[q] = total
                else:
                    t3s[q] = total
                    send(t3s.at[q], t3r.at[q], t2_s.at[q, 0], t2_r.at[q, 0], dev(flip_yl=True))
        else:
            arrived(t1r.at[q, pl.ds(0, 4)], t1_s.at[q, 0], t1_r.at[q, 0])
            for j in range(1, 4):
                t2s[q, at_x(j)] = (mine(q, yl, at_x(j)) + t1r[q, at_x(j)].astype(F32)).astype(BF16)
                send(t2s.at[q, at_x(j)], t2r.at[q, x], t2_s.at[q, j], t2_r.at[q, j], dev(dx=j))
            keep[q] = mine(q, yl, x) + t1r[q, x].astype(F32)

    def finish(q):
        total = keep[q]
        if q % 2 == 0:
            arrived(t3r.at[q], t2_s.at[q, 0], t2_r.at[q, 0])
            total = total + t3r[q]
        else:
            for j in range(1, 4):
                arrived(t2r.at[q, at_x(-j)], t2_s.at[q, j], t2_r.at[q, j])
                total = total + t2r[q, at_x(-j)].astype(F32)
        out[pl.ds(q * 128, 128), :] = total * (1.0 / (32 * LEN))

    steps = dict(
        bhop=bhop, bw=bw, ahop=ahop, aw=aw, by=by, byw=byw, ay=ay, ayw=ayw, g=gsend, gw=gw,
        py=py, px=px, pr=pr, pc=pc, pw=pw, bs=bs, br=br, bl=bl,
        rot=rot, st=st, own=own, sq=squares, spr=spread, mid=middle, fin=finish,
    )
    for name, *what in WORK:
        steps[name](*what)
    for copy in pending:
        copy.wait_send()


def shards(acts, out_grads, basis_out, basis_in, slot_sequence, seq_lengths):
    sem = pltpu.SemaphoreType.DMA
    any_, smem = pl.BlockSpec(memory_space=pl.ANY), pl.BlockSpec(memory_space=pltpu.SMEM)
    pair = lambda *shape: [sem(shape)] * 2
    return pl.pallas_call(
        kernel,
        name="eigenvalues",
        out_shape=jax.ShapeDtypeStruct((512, 128), F32),
        in_specs=[any_] * 4 + [smem] * 2,
        out_specs=pl.BlockSpec(memory_space=pltpu.VMEM),
        scratch_shapes=[
            pltpu.VMEM((2, 512, 512), BF16),
            pltpu.VMEM((8, 512, 512), BF16),
            pltpu.VMEM((8, 512, 512), BF16),
            pltpu.VMEM((2, 8, 512, 128), BF16),
            pltpu.VMEM((8, 2, 8, 128, 256), BF16),
            pltpu.VMEM((8, 512, 256), BF16),
            pltpu.VMEM((8, 512, 256), F32),
            pltpu.VMEM((2, 4, QS, 512, 128), BF16),
            pltpu.VMEM((2, 4, QS, 512, 128), BF16),
            pltpu.VMEM((512, 512), F32),
            pltpu.VMEM((QS, 2, 8, 128, 128), F32),
            pltpu.VMEM((QS, 8, 128, 128), F32),
            pltpu.VMEM((QS, 128, 128), F32),
            pltpu.VMEM((QS, 8, 128, 128), BF16),
            pltpu.VMEM((QS, 8, 128, 128), BF16),
            pltpu.VMEM((QS, 4, 128, 128), BF16),
            pltpu.VMEM((QS, 4, 128, 128), BF16),
            pltpu.VMEM((QS, 128, 128), F32),
            pltpu.VMEM((QS, 128, 128), F32),
            sem((11,)),
            *[sem, sem],
            *pair(8), *pair(4, 4), *pair(4),
            *pair(2, 2, 4), *[sem, sem], *pair(2, 4), *[sem, sem],
            *pair(2, 4), *pair(2, 4), *pair(2, 4, QS), *pair(QS), *pair(QS, 4), *pair(QS, 4),
        ],
        compiler_params=pltpu.CompilerParams(
            collective_id=0, has_side_effects=True, vmem_limit_bytes=56 << 20
        ),
        cost_estimate=pl.CostEstimate(flops=10 * 2**30, bytes_accessed=12 << 20, transcendentals=0),
    )(acts, out_grads, basis_out, basis_in, slot_sequence, seq_lengths)


def solution(mesh):
    return jax.shard_map(
        shards,
        mesh=mesh,
        in_specs=(
            P("dp", "tensor"),
            P("dp", "tensor"),
            P("tensor", None),
            P("tensor", None),
            P(),
            P(),
        ),
        out_specs=P("tensor", "dp"),
        check_vma=False,
    )
```

```python
import jax
import jax.numpy as jnp
from jax import lax
from jax.experimental import pallas as pl
from jax.experimental.pallas import tpu as pltpu
from jax.sharding import PartitionSpec as P

LEN = 256
MESH = pl.DeviceIdType.MESH
F32, BF16 = jnp.float32, jnp.bfloat16
ORDER = (4, 3, -3, 2, -2, 1, -1, 0)
GROUPS = ((0, 1), (1, 3), (3, 5), (5, 8))
QS = 4
WORK = (
    ("py", 0), ("bhop", 1), ("py", 1), ("ahop", 0, 1), ("py", 2), ("ay",), ("bw", 1), ("bhop", 2), ("px", 0),
    ("px", 1), ("g",), ("bw", 2), ("bhop", 3), ("aw", 0, 1), ("ahop", 0, 2), ("px", 2), ("bw", 3),
    ("bhop", 4), ("pr", 0), ("ayw",), ("ahop", 1, 1), ("pr", 1), ("py", 3), ("pr", 2), ("aw", 0, 2),
    ("ahop", 0, 3), ("bw", 4), ("bs", 0), ("by",), ("aw", 1, 1), ("pc", 0), ("ahop", 1, 2), ("pw", 0),
    ("aw", 0, 3), ("ahop", 0, 4), ("gw",), ("st", 0, 0), ("pc", 1), ("st", 0, 1), ("px", 3), ("aw", 1, 2),
    ("ahop", 1, 3), ("pw", 1), ("st", 1, 0), ("pc", 2), ("pr", 3), ("st", 1, 1), ("byw",), ("bs", 1),
    ("br", 0), ("aw", 1, 3), ("aw", 0, 4), ("pw", 2), ("st", 2, 0), ("ahop", 1, 4), ("rot", 0, 0), ("pc", 3),
    ("pw", 3), ("st", 2, 1), ("rot", 2, 0), ("st", 3, 0), ("br", 1), ("rot", 1, 0), ("own",), ("aw", 1, 4),
    ("rot", 1, 1), ("st", 3, 1), ("bl", 0), ("rot", 2, 1), ("rot", 0, 1), ("bl", 1), ("rot", 3, 0),
    ("rot", 3, 1), ("sq", 1), ("sq", 2), ("sq", 0), ("sq", 3), ("spr", 1), ("spr", 2), ("spr", 3), ("spr", 0),
    ("mid", 1), ("mid", 2), ("mid", 3), ("mid", 0), ("fin", 1), ("fin", 2), ("fin", 3), ("fin", 0),
)


def kernel(
    acts, grads, bout, bin_, slot_seq, seq_len, out,
    g, bo, bp, a, bi, ra, acc, sb, rb, ownp, sq, cr, keep, t1s, t1r, t2s, t2r, t3s, t3r,
    loc, g_s, g_r, py_s, py_r, px_s, px_r, pc_s, pc_r,
    az_s, az_r, ay_s, ay_r, bz_s, bz_r, by_s, by_r,
    bx_s, bx_r, bc_s, bc_r, rs_s, rs_r, cs_s, cs_r, t1_s, t1_r, t2_s, t2_r,
):
    d, t = lax.axis_index("dp"), lax.axis_index("tensor")
    yl, x, c = d // 8, (d // 2) % 4, d % 2
    z, yh = t // 2, t % 2

    def dev(dx=0, dz=0, flip_yl=False, flip_c=False, flip_yh=False):
        nyl = 1 - yl if flip_yl else yl
        nc = 1 - c if flip_c else c
        nyh = 1 - yh if flip_yh else yh
        return (nyl * 8 + (x + dx + 4) % 4 * 2 + nc, (z + dz + 8) % 8 * 2 + nyh)

    def remote(src, dst, s, r, to):
        return pltpu.make_async_remote_copy(
            src_ref=src, dst_ref=dst, send_sem=s, recv_sem=r,
            device_id=to, device_id_type=MESH,
        )

    pending = []

    def send(src, dst, s, r, to):
        copy = remote(src, dst, s, r, to)
        copy.start()
        pending.append(copy)

    def arrived(dst, s, r):
        remote(dst, dst, s, r, dev(dz=1)).wait_recv()

    def way(i):
        return 1 - 2 * i

    neighbour = dev(flip_yl=True, flip_yh=True)
    partners = [dev(dz=1), dev(dz=-1), dev(flip_yh=True), neighbour, dev(flip_c=True)]
    partners += [dev(dx=j) for j in range(1, 4)] + [dev(flip_yl=True)]
    barrier = pltpu.get_barrier_semaphore()
    for to in partners:
        pl.semaphore_signal(barrier, inc=1, device_id=to, device_id_type=MESH)

    def column(k, h):
        return pl.multiple_of(((z + ORDER[k] + 8) % 8 * 2 + h) * 512, 512)

    me = x * 2 + c
    my_cols = pl.multiple_of(me * 256, 256)
    local = [
        pltpu.make_async_copy(acts, a.at[yh, z], loc.at[8]),
        pltpu.make_async_copy(bin_.at[:, pl.ds(my_cols, 256)], bi.at[me, yh, z], loc.at[9]),
        pltpu.make_async_copy(grads, g.at[0], loc.at[10]),
    ]
    local += [pltpu.make_async_copy(bout.at[:, pl.ds(column(k, yh), 512)], bo.at[k], loc.at[k]) for k in range(8)]
    for copy in local[:2]:
        copy.start()
    pl.semaphore_wait(barrier, len(partners))

    def half(ref, i, rows, h):
        return ref.at[pl.ds(rows * i, rows)] if h == 4 else ref

    def bhop(h):
        for i in range(2):
            origin = (z - way(i) * (h - 1) + 8) % 8
            src = bi.at[me, yh, origin] if h > 1 else bin_.at[:, pl.ds(my_cols, 256)]
            send(half(src, i, 64, h), half(bi.at[me, yh, origin], i, 64, h), bz_s.at[i, h - 1], bz_r.at[i, h - 1], dev(dz=way(i)))

    def bw(h):
        for i in range(2):
            ref = half(bi.at[me, yh, (z - way(i) * h + 8) % 8], i, 64, h)
            arrived(ref, bz_s.at[i, h - 1], bz_r.at[i, h - 1])
        if h == 1:
            for copy in local[2:]:
                copy.start()
        if h == 4:
            local[1].wait()

    def ahop(u, h):
        side = 1 - yh if u else yh
        for i in range(2):
            origin = (z - way(i) * (h - 1) + 8) % 8
            dst = half(a.at[side, origin], i, 256, h)
            src = acts if h == 1 and u == 0 else dst
            send(src, dst, az_s.at[u, i, h - 1], az_r.at[u, i, h - 1], dev(dz=way(i)))

    def aw(u, h):
        side = 1 - yh if u else yh
        for i in range(2):
            ref = half(a.at[side, (z - way(i) * h + 8) % 8], i, 256, h)
            arrived(ref, az_s.at[u, i, h - 1], az_r.at[u, i, h - 1])
        if u == 0 and h == 4:
            local[0].wait()

    def by():
        ref = bi.at[me, yh]
        send(ref, ref, by_s, by_r, neighbour)

    def byw():
        arrived(bi.at[me, 1 - yh], by_s, by_r)

    def ay():
        send(acts, a.at[yh, z], ay_s, ay_r, dev(flip_yh=True))

    def ayw():
        arrived(a.at[1 - yh, z], ay_s, ay_r)

    def gsend():
        send(grads, g.at[1], g_s, g_r, dev(flip_yh=True))

    def gw():
        arrived(g.at[1], g_s, g_r)
        for copy in local[2:]:
            copy.wait()

    def rows(dx):
        return pl.multiple_of(c * 256 + (x + dx + 4) % 4 * 64, 64)

    def span(n):
        return pl.ds(GROUPS[n][0], GROUPS[n][1] - GROUPS[n][0])

    def py(n):
        for k in range(*GROUPS[n]):
            row, cut = rows(0), pl.ds(column(k, 1 - yh), 512)
            send(bout.at[pl.ds(row, 64), cut], bp.at[k, pl.ds(row, 64)], py_s.at[k], py_r.at[k], neighbour)

    def px(n):
        for k in range(*GROUPS[n]):
            arrived(bp.at[k, pl.ds(rows(0), 64)], py_s.at[k], py_r.at[k])
        ref = bp.at[span(n), pl.ds(rows(0), 64)]
        for i in range(2):
            send(ref, ref, px_s.at[n, i], px_r.at[n, i], dev(dx=way(i)))

    def pr(n):
        for i in range(2):
            row = rows(-way(i))
            arrived(bp.at[span(n), pl.ds(row, 64)], px_s.at[n, i], px_r.at[n, i])
            ref = bp.at[span(n), pl.ds(row + 32 * i, 32)]
            send(ref, ref, px_s.at[n, 2 + i], px_r.at[n, 2 + i], dev(dx=way(i)))

    def pc(n):
        for i in range(2):
            arrived(bp.at[span(n), pl.ds(rows(2) + 32 * i, 32)], px_s.at[n, 2 + i], px_r.at[n, 2 + i])
        ref = bp.at[span(n), pl.ds(pl.multiple_of(c * 256, 256), 256)]
        send(ref, ref, pc_s.at[n], pc_r.at[n], dev(flip_c=True))

    def pw(n):
        arrived(bp.at[span(n), pl.ds(pl.multiple_of((1 - c) * 256, 256), 256)], pc_s.at[n], pc_r.at[n])

    def block(dx, e):
        return (x + dx + 4) % 4 * 2 + e

    def b_part(dx, e, u):
        return bi.at[block(dx, e), 1 - yh if u else yh]

    def to_core(dx, u, n):
        ref = b_part(dx, c, u)
        send(ref, ref, bc_s.at[u, n], bc_r.at[u, n], dev(flip_c=True))

    def bs(u):
        ref = b_part(0, c, u)
        for i in range(2):
            send(ref, ref, bx_s.at[u, i], bx_r.at[u, i], dev(dx=way(i)))
        to_core(0, u, 0)

    def br(u):
        for i in range(2):
            ref = b_part(-way(i), c, u)
            arrived(ref, bx_s.at[u, i], bx_r.at[u, i])
            part = ref.at[pl.ds(4 * i, 4)]
            send(part, part, bx_s.at[u, 2 + i], bx_r.at[u, 2 + i], dev(dx=way(i)))
            to_core(-way(i), u, 1 + i)

    def bl(u):
        for i in range(2):
            arrived(b_part(2, c, u).at[pl.ds(4 * i, 4)], bx_s.at[u, 2 + i], bx_r.at[u, 2 + i])
        to_core(2, u, 3)

    def rot_half(b, h):
        left = jnp.concatenate([a[h, k] for k in range(8)], axis=1)
        return jnp.dot(left, bi[b, h].reshape(1024, 256), preferred_element_type=F32)

    def rot(n, u):
        dx = (0, -1, 1, 2)[n]
        for e in (c, 1 - c):
            b = block(dx, e)
            if e is not c:
                arrived(b_part(dx, e, u), bc_s.at[u, n], bc_r.at[u, n])
            if u == 0:
                acc[b] = rot_half(b, yh)
            else:
                total = acc[b] + rot_half(b, 1 - yh)
                place = lax.broadcasted_iota(jnp.int32, (LEN, 256), 0)
                for slot in range(2):
                    count = seq_len[slot_seq[d * 2 + slot]]
                    part = total[slot * LEN : (slot + 1) * LEN]
                    ra[b, pl.ds(slot * LEN, LEN), :] = jnp.where(place < count, part, 0.0).astype(BF16)

    def product(k, pair):
        cut = pl.ds(pair * 256, 256)
        own = jnp.dot(g[0], bo[k, :, cut], preferred_element_type=F32)
        return own + jnp.dot(g[1], bp[k, :, cut], preferred_element_type=F32)

    def rs_part(ref, i, s, q):
        return ref.at[0, s, q, pl.ds(256 * i, 256)] if s == 0 else ref.at[i, s, q]

    def rs_send(i, s, q):
        send(rs_part(sb, i, s, q), rs_part(rb, i, s, q), rs_s.at[i, s, q], rs_r.at[i, s, q], dev(dz=way(i)))

    def rs_arrived(i, s, q):
        arrived(rs_part(rb, i, s, q), rs_s.at[i, s, q], rs_r.at[i, s, q])

    def st(s, pair):
        if s == 0:
            total = product(0, pair)
            for e in range(2):
                sb[0, 0, 2 * pair + e] = total[:, e * 128 : (e + 1) * 128].astype(BF16)
            for i in range(2):
                for e in range(2):
                    rs_send(i, 0, 2 * pair + e)
            return
        for i in range(2):
            total = product(2 * s - 1 + i, pair)
            for e in range(2):
                q, mine = 2 * pair + e, total[:, e * 128 : (e + 1) * 128]
                rs_arrived(i, s - 1, q)
                if s == 1:
                    lo, no = 256 * i, 256 * (1 - i)
                    with_sum = mine[lo : lo + 256] + rb[0, 0, q, pl.ds(lo, 256), :].astype(F32)
                    sb[i, s, q, pl.ds(lo, 256), :] = with_sum.astype(BF16)
                    sb[i, s, q, pl.ds(no, 256), :] = mine[no : no + 256].astype(BF16)
                else:
                    sb[i, s, q] = (mine + rb[i, s - 1, q].astype(F32)).astype(BF16)
                rs_send(i, s, q)

    def own():
        for pair in range(2):
            ownp[:, pl.ds(pair * 256, 256)] = product(7, pair)

    def squares(q):
        for i in range(2):
            rs_arrived(i, 3, q)
        rotated = ownp[:, pl.ds(q * 128, 128)] + rb[0, 3, q].astype(F32) + rb[1, 3, q].astype(F32)
        rotated = rotated.T.astype(BF16)
        for b in range(8):
            total = None
            for slot in range(2):
                rng = slice(slot * LEN, (slot + 1) * LEN)
                r = jnp.dot(rotated[:, rng], ra[b, rng, :], preferred_element_type=F32)
                total = r * r if total is None else total + r * r
            sq[q, 0, b] = total[:, :128]
            sq[q, 1, b] = total[:, 128:]
        send(sq.at[q, 1 - c], cr.at[q], cs_s.at[q], cs_r.at[q], dev(flip_c=True))

    def mine(q, y, x_to):
        b = y * 4 + (x_to + 4) % 4
        return sq[q, c, b] + cr[q, b]

    def at_x(j):
        return (x + j + 4) % 4

    def spread(q):
        arrived(cr.at[q], cs_s.at[q], cs_r.at[q])
        if q % 2 == 0:
            for j in range(1, 4):
                for y in range(2):
                    t1s[q, at_x(j) * 2 + y] = mine(q, y, at_x(j)).astype(BF16)
                send(t1s.at[q, pl.ds(at_x(j) * 2, 2)], t1r.at[q, pl.ds(x * 2, 2)], t1_s.at[q, j], t1_r.at[q, j], dev(dx=j))
        else:
            for k in range(4):
                t1s[q, k] = mine(q, 1 - yl, k).astype(BF16)
            send(t1s.at[q, pl.ds(0, 4)], t1r.at[q, pl.ds(0, 4)], t1_s.at[q, 0], t1_r.at[q, 0], dev(flip_yl=True))

    def middle(q):
        if q % 2 == 0:
            for j in range(1, 4):
                arrived(t1r.at[q, pl.ds(at_x(-j) * 2, 2)], t1_s.at[q, j], t1_r.at[q, j])
            for y in (1 - yl, yl):
                total = mine(q, y, x)
                for j in range(1, 4):
                    total = total + t1r[q, at_x(-j) * 2 + y].astype(F32)
                if y is yl:
                    keep[q] = total
                else:
                    t3s[q] = total
                    send(t3s.at[q], t3r.at[q], t2_s.at[q, 0], t2_r.at[q, 0], dev(flip_yl=True))
        else:
            arrived(t1r.at[q, pl.ds(0, 4)], t1_s.at[q, 0], t1_r.at[q, 0])
            for j in range(1, 4):
                t2s[q, at_x(j)] = (mine(q, yl, at_x(j)) + t1r[q, at_x(j)].astype(F32)).astype(BF16)
                send(t2s.at[q, at_x(j)], t2r.at[q, x], t2_s.at[q, j], t2_r.at[q, j], dev(dx=j))
            keep[q] = mine(q, yl, x) + t1r[q, x].astype(F32)

    def finish(q):
        total = keep[q]
        if q % 2 == 0:
            arrived(t3r.at[q], t2_s.at[q, 0], t2_r.at[q, 0])
            total = total + t3r[q]
        else:
            for j in range(1, 4):
                arrived(t2r.at[q, at_x(-j)], t2_s.at[q, j], t2_r.at[q, j])
                total = total + t2r[q, at_x(-j)].astype(F32)
        out[pl.ds(q * 128, 128), :] = total * (1.0 / (32 * LEN))

    steps = dict(
        bhop=bhop, bw=bw, ahop=ahop, aw=aw, by=by, byw=byw, ay=ay, ayw=ayw, g=gsend, gw=gw,
        py=py, px=px, pr=pr, pc=pc, pw=pw, bs=bs, br=br, bl=bl,
        rot=rot, st=st, own=own, sq=squares, spr=spread, mid=middle, fin=finish,
    )
    for name, *what in WORK:
        steps[name](*what)
    for copy in pending:
        copy.wait_send()


def shards(acts, out_grads, basis_out, basis_in, slot_sequence, seq_lengths):
    sem = pltpu.SemaphoreType.DMA
    any_, smem = pl.BlockSpec(memory_space=pl.ANY), pl.BlockSpec(memory_space=pltpu.SMEM)
    pair = lambda *shape: [sem(shape)] * 2
    return pl.pallas_call(
        kernel,
        name="eigenvalues",
        out_shape=jax.ShapeDtypeStruct((512, 128), F32),
        in_specs=[any_] * 4 + [smem] * 2,
        out_specs=pl.BlockSpec(memory_space=pltpu.VMEM),
        scratch_shapes=[
            pltpu.VMEM((2, 512, 512), BF16),
            pltpu.VMEM((8, 512, 512), BF16),
            pltpu.VMEM((8, 512, 512), BF16),
            pltpu.VMEM((2, 8, 512, 128), BF16),
            pltpu.VMEM((8, 2, 8, 128, 256), BF16),
            pltpu.VMEM((8, 512, 256), BF16),
            pltpu.VMEM((8, 512, 256), F32),
            pltpu.VMEM((2, 4, QS, 512, 128), BF16),
            pltpu.VMEM((2, 4, QS, 512, 128), BF16),
            pltpu.VMEM((512, 512), F32),
            pltpu.VMEM((QS, 2, 8, 128, 128), F32),
            pltpu.VMEM((QS, 8, 128, 128), F32),
            pltpu.VMEM((QS, 128, 128), F32),
            pltpu.VMEM((QS, 8, 128, 128), BF16),
            pltpu.VMEM((QS, 8, 128, 128), BF16),
            pltpu.VMEM((QS, 4, 128, 128), BF16),
            pltpu.VMEM((QS, 4, 128, 128), BF16),
            pltpu.VMEM((QS, 128, 128), F32),
            pltpu.VMEM((QS, 128, 128), F32),
            sem((11,)),
            *[sem, sem],
            *pair(8), *pair(4, 4), *pair(4),
            *pair(2, 2, 4), *[sem, sem], *pair(2, 4), *[sem, sem],
            *pair(2, 4), *pair(2, 4), *pair(2, 4, QS), *pair(QS), *pair(QS, 4), *pair(QS, 4),
        ],
        compiler_params=pltpu.CompilerParams(
            collective_id=0, has_side_effects=True, vmem_limit_bytes=56 << 20
        ),
        cost_estimate=pl.CostEstimate(flops=10 * 2**30, bytes_accessed=12 << 20, transcendentals=0),
    )(acts, out_grads, basis_out, basis_in, slot_sequence, seq_lengths)


def solution(mesh):
    return jax.shard_map(
        shards,
        mesh=mesh,
        in_specs=(
            P("dp", "tensor"),
            P("dp", "tensor"),
            P("tensor", None),
            P("tensor", None),
            P(),
            P(),
        ),
        out_specs=P("tensor", "dp"),
        check_vma=False,
    )
```
